32 devices in a mesh: tm: 8 (over y, x, core), space: 4 (over z).
Axes of the slice: x: 2, y: 2, z: 4, core: 2. Of those that a mesh axis runs over, the one named last changes fastest.
Arguments:
- tokens: bfloat16 [32, 12, 80, 1024], P('tm', 'space'), may hold values from -6 to 6
- w_in: bfloat16 [1024, 4416], replicated, may hold values from -0.1875 to 0.1875
- w_out: bfloat16 [2048, 1024], replicated, may hold values from -0.125 to 0.125
- a_log_time: float32 [32], replicated, may hold values from -16 to -3
- a_log_space: float32 [32], replicated, may hold values from -14 to -3
- dt_bias_time: float32 [32], replicated, may hold values from -1 to 1
- dt_bias_space: float32 [32], replicated, may hold values from -1 to 1
- skip_time: float32 [32], replicated, may hold values from 0.5 to 1.5
- skip_space: float32 [32], replicated, may hold values from 0.5 to 1.5
- norm_gain: float32 [2048], replicated, may hold values from 0.25 to 1.75
Outputs:
- mixed: bfloat16 [32, 12, 80, 1024], P('tm', 'space')
The draws below stay inside these ranges and needn't reach their ends.
All inputs are finite; a program needn't handle non-finite values.
Results may differ from the reference program's by a relative error of at most 0.0062.
The reference program's roundings to bfloat16 on the way count: a program that leaves them out, or rounds other values in their place, can miss the bound.
Values may be sent and summed in bfloat16 or wider, within the bound.
No kernel may reach another device: no remote copies, remote signals or barrier semaphores. Data moves between devices by JAX's collectives and lax.ppermute only.
A program may use at most 192 MiB of HBM per device.

```python
import jax
import jax.numpy as jnp
from jax import lax

D = 1024
HEADS = 32
HEAD_DIM = 64
STATE = 64
COLS = 80
DI = 2048
NPROJ = 4416
FRAMES = 32
ROWS = 12


def level_of(own_key, extent, pieces, smallest, high):
    factor_of = 1.0
    for position, shards_of in pieces:
        heights = jax.random.uniform(jax.random.fold_in(jax.random.fold_in(own_key, 6), position), (shards_of,), jnp.float32, smallest / len(pieces), high / len(pieces))
        factor_of = factor_of * jnp.repeat(jnp.exp(heights), extent[position] // shards_of).reshape((-1,) + (1,) * (len(extent) - 1 - position))
    return factor_of


def noise(own_key, dims, scale, bound, cuts=(), kind=jnp.bfloat16):
    drawn = scale * jax.random.normal(own_key, dims, jnp.float32)
    if cuts:
        drawn = drawn * level_of(own_key, dims, cuts, -0.22, 0.18)
    return jnp.clip(drawn, -bound, bound).astype(kind)


def setup_inputs(seed: int = 0) -> dict:
    streams_of = jax.random.split(jax.random.key(seed), 11)
    tokens = noise(streams_of[0], (FRAMES, ROWS, COLS, D), 1.0, 6.0, ((0, 8), (1, 4)))
    w_in = noise(streams_of[1], (D, NPROJ), D ** -0.5, 0.1875)
    w_out = noise(streams_of[2], (DI, D), DI ** -0.5, 0.125)
    a_log_time = jnp.clip(jax.random.uniform(streams_of[3], (HEADS,), jnp.float32, -16.0, -3.0), -16.0, -3.0)
    a_log_space = jnp.clip(jax.random.uniform(streams_of[4], (HEADS,), jnp.float32, -14.0, -3.0), -14.0, -3.0)
    dt_bias_time = jnp.clip(jax.random.uniform(streams_of[5], (HEADS,), jnp.float32, -1.0, 1.0), -1.0, 1.0)
    dt_bias_space = jnp.clip(jax.random.uniform(streams_of[6], (HEADS,), jnp.float32, -1.0, 1.0), -1.0, 1.0)
    skip_time = jnp.clip(jax.random.uniform(streams_of[7], (HEADS,), jnp.float32, 0.5, 1.5), 0.5, 1.5)
    skip_space = jnp.clip(jax.random.uniform(streams_of[8], (HEADS,), jnp.float32, 0.5, 1.5), 0.5, 1.5)
    norm_gain = jnp.clip(1.0 + 0.15 * jax.random.normal(streams_of[9], (DI,), jnp.float32), 0.25, 1.75)
    return {"tokens": tokens, "w_in": w_in, "w_out": w_out, "a_log_time": a_log_time, "a_log_space": a_log_space, "dt_bias_time": dt_bias_time, "dt_bias_space": dt_bias_space, "skip_time": skip_time, "skip_space": skip_space, "norm_gain": norm_gain}


def split_pieces(projected):
    base = 2 * DI
    gate_z = projected[:, :DI].astype(jnp.bfloat16)
    inner_x = projected[:, DI:base].astype(jnp.bfloat16)
    b_time = projected[:, base:base + STATE].astype(jnp.bfloat16)
    c_time = projected[:, base + STATE:base + 2 * STATE].astype(jnp.bfloat16)
    b_space = projected[:, base + 2 * STATE:base + 3 * STATE].astype(jnp.bfloat16)
    c_space = projected[:, base + 3 * STATE:base + 4 * STATE].astype(jnp.bfloat16)
    raw_time = projected[:, base + 4 * STATE:base + 4 * STATE + HEADS].astype(jnp.bfloat16)
    raw_space = projected[:, base + 4 * STATE + HEADS:base + 4 * STATE + 2 * HEADS]
    return (gate_z, inner_x, b_time, c_time, b_space, c_space, raw_time, raw_space)

def local_scan(inner_seq, inject, readout, log_decay, step_size):
    signal = inner_seq.astype(jnp.float32)
    inject_wide = inject.astype(jnp.float32)
    readout_wide = readout.astype(jnp.float32)
    cum_decay = jnp.cumsum(log_decay, axis=0)
    scores = jnp.dot(readout_wide, inject_wide.T, precision=lax.Precision.HIGHEST)
    log_span = cum_decay[:, None, :] - cum_decay[None, :, :]
    length = log_decay.shape[0]
    causal = jnp.arange(length)[:, None] >= jnp.arange(length)[None, :]
    decay_mask = jnp.where(causal[:, :, None], jnp.exp(jnp.minimum(log_span, 0.0)), 0.0)
    weights = decay_mask * scores[:, :, None] * step_size[None, :, :]
    local_out = jnp.einsum('srh,rhp->shp', weights, signal, precision=lax.Precision.HIGHEST)
    tail_weight = jnp.exp(cum_decay[-1][None, :] - cum_decay) * step_size
    end_state = jnp.einsum('rhp,rn->hpn', tail_weight[:, :, None] * signal, inject_wide, precision=lax.Precision.HIGHEST)
    return (local_out, end_state, cum_decay[-1], cum_decay)

def apply_start(local_out, cum_decay, readout, inner_seq, skip_gain, start_state):
    carried = jnp.einsum('sn,hpn->shp', readout.astype(jnp.float32), start_state, precision=lax.Precision.HIGHEST)
    return local_out + jnp.exp(cum_decay)[:, :, None] * carried + skip_gain[None, :, None] * inner_seq.astype(jnp.float32)

def stretch_full(inner_seq, inject, readout, log_decay, step_size, skip_gain, start_state):
    local_out, end_state, total_decay, cum_decay = local_scan(inner_seq, inject, readout, log_decay, step_size)
    result = apply_start(local_out, cum_decay, readout, inner_seq, skip_gain, start_state)
    return (result, jnp.exp(total_decay)[:, None, None] * start_state + end_state)

def reference(tokens, w_in, w_out, a_log_time, a_log_space, dt_bias_time, dt_bias_space, skip_time, skip_space, norm_gain):

    def project_frame(frame_tok):
        projected = jnp.dot(frame_tok.reshape(-1, D), w_in, preferred_element_type=jnp.float32)
        return split_pieces(projected)
    gate_z, inner_x, b_time, c_time, b_space, c_space, raw_time, raw_space = lax.map(project_frame, tokens)
    step_time = jax.nn.softplus(raw_time.astype(jnp.float32) + dt_bias_time)
    step_space = jax.nn.softplus(raw_space + dt_bias_space)
    decay_time = -jnp.exp(a_log_time) * step_time
    decay_space = -jnp.exp(a_log_space) * step_space

    def on_grid(values):
        return values.reshape((FRAMES, ROWS, COLS) + values.shape[2:])

    def by_rows(values):
        return jnp.swapaxes(values, 0, 1)
    inner_grid = inner_x.reshape(FRAMES, ROWS, COLS, HEADS, HEAD_DIM)
    run_rows = jax.vmap(stretch_full, in_axes=(0, 0, 0, 0, 0, None, 0))

    def time_row(row_in):
        reordered = [jnp.swapaxes(values, 0, 1) for values in row_in]
        zero_start = jnp.zeros((COLS, HEADS, HEAD_DIM, STATE), jnp.float32)
        result, unused_end = run_rows(reordered[0], reordered[1], reordered[2], reordered[3], reordered[4], skip_time, zero_start)
        return jnp.swapaxes(result.astype(jnp.bfloat16), 0, 1)
    time_rows = lax.map(time_row, (by_rows(inner_grid), by_rows(on_grid(b_time)), by_rows(on_grid(c_time)), by_rows(on_grid(decay_time)), by_rows(on_grid(step_time))))

    def space_step(carried_state, row_in):
        inner_seq, inject, readout, log_decay, step_size, gate_row = row_in
        result, next_state = run_rows(inner_seq, inject, readout, log_decay, step_size, skip_space, carried_state)
        gated = result.reshape(FRAMES, COLS, DI) * jax.nn.silu(gate_row.astype(jnp.float32))
        inv_scale = lax.rsqrt(lax.optimization_barrier(jnp.mean(gated * gated, axis=-1, keepdims=True)) + 1e-05)
        return (next_state, (gated * inv_scale * norm_gain).astype(jnp.bfloat16))
    space_init = jnp.zeros((FRAMES, HEADS, HEAD_DIM, STATE), jnp.float32)
    unused_last, normed = lax.scan(space_step, space_init, (time_rows, by_rows(on_grid(b_space)), by_rows(on_grid(c_space)), by_rows(on_grid(decay_space)), by_rows(on_grid(step_space)), by_rows(on_grid(gate_z))))
    normed = jnp.swapaxes(normed, 0, 1)

    def finish_frame(frame_in):
        normed_frame, token_frame = frame_in
        summed = jnp.dot(normed_frame.reshape(-1, DI), w_out, preferred_element_type=jnp.float32)
        summed = summed + token_frame.reshape(-1, D).astype(jnp.float32)
        return summed.astype(jnp.bfloat16).reshape(ROWS, COLS, D)
    return lax.map(finish_frame, (normed, tokens))
```

```python
import functools

import jax
import jax.numpy as jnp
from jax import lax
from jax.experimental import pallas as pl
from jax.experimental.pallas import tpu as pltpu
from jax.sharding import PartitionSpec as P

D = 1024
HEADS = 32
HEAD_DIM = 64
STATE = 64
DI = 2048
BLK = 16
QUAD = 256
LANES = 128
LOG2E = 1.4426950408889634
TOP = 64.0
GROUPS = (8, 8, 8, 8)
BF = jnp.bfloat16
F32 = jnp.float32
VMEM = 56 * 1024 * 1024


def call(kernel, name, grid, in_specs, out_specs, out_shape, flops, moved, scratch=()):
    return pl.pallas_call(
        kernel,
        name=name,
        grid=grid,
        in_specs=in_specs,
        out_specs=out_specs,
        out_shape=out_shape,
        scratch_shapes=scratch,
        compiler_params=pltpu.CompilerParams(vmem_limit_bytes=VMEM),
        cost_estimate=pl.CostEstimate(flops=flops, bytes_accessed=moved, transcendentals=0),
    )


def dot(a, b):
    return jnp.dot(a, b, preferred_element_type=F32)


def dot_nt(a, b):
    return lax.dot_general(a, b, (((1,), (1,)), ((), ())), preferred_element_type=F32)


def dot_tn(a, b):
    return lax.dot_general(a, b, (((0,), (0,)), ((), ())), preferred_element_type=F32)


def softplus(x):
    return jnp.maximum(x, 0.0) + jnp.log1p(jnp.exp(-jnp.abs(x)))


def split2(v):
    high = v.astype(BF)
    return high, (v - high.astype(F32)).astype(BF)


def full(shape):
    return pl.BlockSpec(shape, lambda *_: (0,) * len(shape))


def arrange_kernel(n, spare, x_ref, o_ref):
    o_ref[:, 0, 0] = x_ref[0].reshape(n, BLK, D)
    if spare:

        @pl.when(pl.program_id(0) == pl.num_programs(0) - 1)
        def _():
            o_ref[n - spare :, 0, 0] = jnp.zeros((spare, BLK, D), BF)


def arrange(tok, n, m):
    fr, npos, _ = tok.shape
    spare = n * m - npos // BLK
    return call(
        functools.partial(arrange_kernel, n, spare),
        "arrange",
        (m, fr),
        [pl.BlockSpec((1, n * BLK, D), lambda h, f: (f, h, 0))],
        pl.BlockSpec((n, 1, 1, BLK, D), lambda h, f: (0, h, f, 0, 0)),
        jax.ShapeDtypeStruct((n, m, fr, BLK, D), BF),
        0,
        4 * fr * npos * D,
    )(tok)


def gate_kernel(x_ref, w_ref, o_ref):
    o_ref[...] = dot(x_ref[...], w_ref[...]).astype(BF)


def gate_proj(flat, w_in):
    rows = flat.shape[0]
    return call(
        gate_kernel,
        "gate_proj",
        (DI // 512,),
        [full((rows, D)), pl.BlockSpec((D, 512), lambda j: (0, j))],
        pl.BlockSpec((rows, 512), lambda j: (0, j)),
        jax.ShapeDtypeStruct((rows, DI), BF),
        2 * rows * D * DI,
        2 * (rows * D + D * DI + rows * DI),
    )(flat, w_in)


def space_prep_kernel(
    npos, x_ref, w_ref, bias_ref, rate_ref, score_ref, cum_ref, row_ref, tail_ref, ecum_ref, b_ref, c_ref, tot_ref
):
    size = score_ref.shape[1]
    proj = dot(x_ref[0], w_ref[...])
    pad = jnp.zeros((size - npos, LANES), F32)
    bc = jnp.concatenate([proj[:, LANES : 2 * LANES].astype(BF).astype(F32), pad], axis=0)
    b = bc[:, :STATE].astype(BF)
    c = bc[:, STATE:].astype(BF)
    step = softplus(proj[:, 2 * LANES :] + bias_ref[...])
    step = jnp.concatenate([step, pad], axis=0)
    dec = step * rate_ref[...]
    ri = lax.broadcasted_iota(jnp.int32, (size, size), 0)
    ci = lax.broadcasted_iota(jnp.int32, (size, size), 1)
    causal = ri >= ci
    cum = jnp.dot(
        causal.astype(F32), dec, precision=lax.Precision.HIGHEST, preferred_element_type=F32
    )
    total = cum[npos - 1 : npos]
    rowterm = jnp.log2(step) - cum
    score_ref[0] = jnp.where(causal, dot_nt(c, b), 0.0)
    cum_ref[0] = cum
    row_ref[0] = rowterm.T[HEADS : 2 * HEADS]
    tail = jnp.exp2(jnp.minimum(total + rowterm, TOP))
    t_hi, t_lo = split2(tail)
    tail_ref[0, 0] = t_hi
    tail_ref[0, 1] = t_lo
    e_hi, e_lo = split2(jnp.exp2(cum))
    ecum_ref[0, 0] = e_hi
    ecum_ref[0, 1] = e_lo
    b_ref[0] = b
    c_ref[0] = c
    tot_ref[0] = total


def space_prep(tok, w_small, bias, rate, size):
    fr, npos, _ = tok.shape

    def per_frame(shape):
        return pl.BlockSpec((1,) + shape, lambda f: (f,) + (0,) * len(shape))

    shapes = [
        ((size, size), F32),
        ((size, LANES), F32),
        ((HEADS, size), F32),
        ((2, size, LANES), BF),
        ((2, size, LANES), BF),
        ((size, STATE), BF),
        ((size, STATE), BF),
        ((1, LANES), F32),
    ]
    return call(
        functools.partial(space_prep_kernel, npos),
        "space_prep",
        (fr,),
        [per_frame((npos, D)), full(w_small.shape), full((1, LANES)), full((1, LANES))],
        [per_frame(s) for s, _ in shapes],
        [jax.ShapeDtypeStruct((fr,) + s, t) for s, t in shapes],
        2 * fr * npos * D * 384,
        6 * 1024 * 1024,
    )(tok, w_small, bias, rate)


def time_prep_kernel(n, m, fr, x_ref, w_ref, bias_ref, rate_ref, score_ref, cum_ref, row_ref):
    proj = dot(x_ref[...], w_ref[...])
    shape = (n, m, fr, 2, 8, LANES)
    q_rows = n * fr * 8
    bc = proj[:, :LANES].astype(BF).astype(F32).reshape(shape)
    raw = proj[:, 2 * LANES :].astype(BF).astype(F32)
    step = softplus(raw + bias_ref[...])
    dec = (step * rate_ref[...]).reshape(shape)
    step = step.reshape(shape)
    ri = lax.broadcasted_iota(jnp.int32, (q_rows, q_rows), 0)
    ci = lax.broadcasted_iota(jnp.int32, (q_rows, q_rows), 1)
    keep = (ri >= ci) & ((ri & 7) == (ci & 7))
    for h in range(m):
        for e in range(2):
            q = 2 * h + e
            running = jnp.zeros((8, LANES), F32)
            parts = []
            for s in range(n):
                for f in range(fr):
                    running = running + dec[s, h, f, e]
                    parts.append(running)
            cum = jnp.concatenate(parts, axis=0)
            bcq = bc[:, h, :, e].reshape(q_rows, LANES)
            b = bcq[:, :STATE].astype(BF)
            c = bcq[:, STATE:].astype(BF)
            score_ref[q] = jnp.where(keep, dot_nt(c, b), 0.0)
            cum_ref[q] = cum
            rowterm = jnp.log2(step[:, h, :, e].reshape(q_rows, LANES)) - cum
            row_ref[q] = rowterm.T[:HEADS]


def time_prep(tok_t, w_small, bias, rate):
    n, m, fr = tok_t.shape[:3]
    rows = n * m * fr * BLK
    q_rows = n * fr * 8
    flat = tok_t.reshape(rows, D)
    return call(
        functools.partial(time_prep_kernel, n, m, fr),
        "time_prep",
        (1,),
        [full((rows, D)), full(w_small.shape), full((1, LANES)), full((1, LANES))],
        [full((2 * m, q_rows, q_rows)), full((2 * m, q_rows, LANES)), full((2 * m, HEADS, q_rows))],
        [
            jax.ShapeDtypeStruct((2 * m, q_rows, q_rows), F32),
            jax.ShapeDtypeStruct((2 * m, q_rows, LANES), F32),
            jax.ShapeDtypeStruct((2 * m, HEADS, q_rows), F32),
        ],
        2 * rows * D * 384,
        6 * 1024 * 1024,
    )(flat, w_small, bias, rate)


def head_pair(score, cum, row, x_pair, rows_in):
    lane = lax.broadcasted_iota(jnp.int32, (1, LANES), 1)
    left = jnp.where(lane < HEAD_DIM, 1.0, 0.0).astype(BF)
    halves = (x_pair * left, x_pair * (1 - left))
    out = []
    for i in range(rows_in // LANES):
        lo, hi = i * LANES, (i + 1) * LANES
        pieces = []
        for k in range(2):
            col = jnp.broadcast_to(cum[k][lo:hi], (LANES, LANES))
            for j in range(i + 1):
                span = col + row[k][:, j * LANES : (j + 1) * LANES]
                weight = jnp.exp2(jnp.minimum(span, TOP)) * score[lo:hi, j * LANES : (j + 1) * LANES]
                pieces.append(weight.astype(BF))
        left_side = jnp.concatenate(pieces, axis=1)
        right_side = jnp.concatenate([halves[0][:hi], halves[1][:hi]], axis=0)
        out.append(dot(left_side, right_side))
    return jnp.concatenate(out, axis=0)


def time_scan_kernel(n, m, fr, head0, x_ref, w_ref, score_ref, cum_ref, row_ref, skip_ref, o_ref):
    base = head0 + 4 * pl.program_id(0)
    q_rows = n * fr * 8
    x = dot(x_ref[...], w_ref[...]).astype(BF).astype(F32)
    x = x.reshape(n, m, fr, 2, 8, QUAD)
    for h in range(m):
        ys = []
        for e in range(2):
            q = 2 * h + e
            xq = x[:, h, :, e].reshape(q_rows, QUAD)
            xb = xq.astype(BF)
            cum = pltpu.roll(cum_ref[q], LANES - base, 1)
            y = []
            for p in range(2):
                a = p * LANES
                heads = (2 * p, 2 * p + 1)
                y.append(
                    head_pair(
                        score_ref.at[q],
                        [cum[:, k : k + 1] for k in heads],
                        [row_ref[q, pl.ds(base + k, 1), :] for k in heads],
                        xb[:, a : a + LANES],
                        q_rows,
                    )
                )
            y = jnp.concatenate(y, axis=1) + skip_ref[...] * xq
            ys.append(y.reshape(n, fr, 8, QUAD))
        o_ref[:, h] = jnp.concatenate(ys, axis=2).astype(BF)


def time_scan(tok_t, w_in, prep, skip, head0, heads):
    n, m, fr = tok_t.shape[:3]
    rows = n * m * fr * BLK
    q_rows = n * fr * 8
    first = (DI + head0 * HEAD_DIM) // QUAD
    own = head0 * HEAD_DIM // QUAD
    cols = heads * HEAD_DIM
    return call(
        functools.partial(time_scan_kernel, n, m, fr, head0),
        "time_scan",
        (heads // 4,),
        [
            full((rows, D)),
            pl.BlockSpec((D, QUAD), lambda j: (0, first + j)),
            full((2 * m, q_rows, q_rows)),
            full((2 * m, q_rows, LANES)),
            full((2 * m, HEADS, q_rows)),
            pl.BlockSpec((1, QUAD), lambda j: (0, own + j)),
        ],
        pl.BlockSpec((n, m, fr, BLK, QUAD), lambda j: (0, 0, 0, 0, j)),
        jax.ShapeDtypeStruct((n, m, fr, BLK, cols), BF),
        2 * rows * D * cols + 4 * rows * q_rows * cols,
        2 * (rows * D + D * cols + rows * cols) + 2 * 1024 * 1024,
    )(tok_t.reshape(rows, D), w_in, *prep, skip)


def frame_rows(ref, frame):
    n, m, _, _, cols = ref.shape
    return jnp.concatenate([ref[:, h, frame].reshape(n * BLK, cols) for h in range(m)], axis=0)


def end_state_kernel(x_ref, tail_ref, b_ref, spread_ref, o_ref):
    spread = spread_ref[...]
    for f in range(x_ref.shape[2]):
        x = frame_rows(x_ref, f).astype(F32)
        wide = dot(tail_ref[f, 0], spread) + dot(tail_ref[f, 1], spread)
        o_ref[f] = dot_tn(b_ref[f], (x * wide).astype(BF)).astype(BF)


def end_state(time_out, tail, b, spread, head0):
    n, m, fr, _, cols = time_out.shape
    size = b.shape[1]
    own = head0 * HEAD_DIM // QUAD
    return call(
        end_state_kernel,
        "end_state",
        (cols // QUAD,),
        [
            pl.BlockSpec((n, m, fr, BLK, QUAD), lambda j: (0, 0, 0, 0, j)),
            full(tail.shape),
            full(b.shape),
            pl.BlockSpec((LANES, QUAD), lambda j: (0, own + j)),
        ],
        pl.BlockSpec((fr, STATE, QUAD), lambda j: (0, 0, j)),
        jax.ShapeDtypeStruct((fr, STATE, cols), BF),
        2 * fr * size * cols * (STATE + 2 * LANES),
        2 * fr * size * cols + 1024 * 1024,
    )(time_out, tail, b, spread)


def local_kernel(head0, npos, x_ref, score_ref, cum_ref, row_ref, skip_ref, o_ref):
    base = head0 + 4 * pl.program_id(1)
    size = score_ref.shape[1]
    xb = frame_rows(x_ref, 0)
    cum = pltpu.roll(cum_ref[0], LANES - HEADS - base, 1)
    y = []
    for p in range(2):
        a = p * LANES
        heads = (2 * p, 2 * p + 1)
        y.append(
            head_pair(
                score_ref.at[0],
                [cum[:, k : k + 1] for k in heads],
                [row_ref[0, pl.ds(base + k, 1), :] for k in heads],
                xb[:, a : a + LANES],
                size,
            )
        )
    y = jnp.concatenate(y, axis=1) + skip_ref[...] * xb.astype(F32)
    o_ref[0] = y[:npos]


def local_scan(time_out, score, cum, row, skip, head0, npos):
    n, m, fr, _, cols = time_out.shape
    size = score.shape[1]
    own = head0 * HEAD_DIM // QUAD
    return call(
        functools.partial(local_kernel, head0, npos),
        "local_scan",
        (fr, cols // QUAD),
        [
            pl.BlockSpec((n, m, 1, BLK, QUAD), lambda f, j: (0, 0, f, 0, j)),
            pl.BlockSpec((1, size, size), lambda f, j: (f, 0, 0)),
            pl.BlockSpec((1, size, LANES), lambda f, j: (f, 0, 0)),
            pl.BlockSpec((1, HEADS, size), lambda f, j: (f, 0, 0)),
            pl.BlockSpec((1, QUAD), lambda f, j: (0, own + j)),
        ],
        pl.BlockSpec((1, npos, QUAD), lambda f, j: (f, 0, j)),
        jax.ShapeDtypeStruct((fr, npos, cols), F32),
        4 * fr * size * size * cols,
        6 * fr * size * cols + 2 * 1024 * 1024,
    )(time_out, score, cum, row, skip)


def gated_of(npos, local_ref, z_ref, ecum_ref, c_ref, spread_ref, prev_ref, states):
    state = states[0][0].astype(F32)
    if len(states) > 1:
        state = state + states[1][0].astype(F32) + prev_ref[0] * states[2][0].astype(F32)
    carried = dot(c_ref[0], state.astype(BF))[:npos]
    spread = spread_ref[...]
    wide = (dot(ecum_ref[0, 0], spread) + dot(ecum_ref[0, 1], spread))[:npos]
    z = z_ref[0].astype(F32)
    return (local_ref[0] + wide * carried) * (z * jax.nn.sigmoid(z))


def lane_sums(v):
    return sum(v[:, a : a + LANES] for a in range(0, v.shape[1], LANES))


def finish_kernel(npos, local_ref, z_ref, ecum_ref, c_ref, spread_ref, prev_ref, gain_ref, *rest):
    *states, o_ref, sq_ref = rest
    gated = gated_of(npos, local_ref, z_ref, ecum_ref, c_ref, spread_ref, prev_ref, states)
    o_ref[0] = (gated * gain_ref[...]).astype(BF)
    part = lane_sums(gated * gated)

    @pl.when(pl.program_id(1) == 0)
    def _():
        sq_ref[0] = part

    @pl.when(pl.program_id(1) > 0)
    def _():
        sq_ref[0] = sq_ref[0] + part


def finish(local, gate, ecum, c, spread, prev, gain, states, head0):
    fr, npos, cols = local.shape
    size = c.shape[1]
    own = head0 * HEAD_DIM // QUAD
    state_spec = pl.BlockSpec((1, STATE, QUAD), lambda f, j: (f, 0, j))
    return call(
        functools.partial(finish_kernel, npos),
        "finish",
        (fr, cols // QUAD),
        [
            pl.BlockSpec((1, npos, QUAD), lambda f, j: (f, 0, j)),
            pl.BlockSpec((1, npos, QUAD), lambda f, j: (f, 0, own + j)),
            pl.BlockSpec((1, 2, size, LANES), lambda f, j: (f, 0, 0, 0)),
            pl.BlockSpec((1, size, STATE), lambda f, j: (f, 0, 0)),
            pl.BlockSpec((LANES, QUAD), lambda f, j: (0, own + j)),
            pl.BlockSpec((1, 1, QUAD), lambda f, j: (f, 0, own + j)),
            pl.BlockSpec((1, QUAD), lambda f, j: (0, own + j)),
        ]
        + [state_spec] * len(states),
        [
            pl.BlockSpec((1, npos, QUAD), lambda f, j: (f, 0, j)),
            pl.BlockSpec((1, npos, LANES), lambda f, j: (f, 0, 0)),
        ],
        [
            jax.ShapeDtypeStruct((fr, npos, cols), BF),
            jax.ShapeDtypeStruct((fr, npos, LANES), F32),
        ],
        2 * fr * size * cols * (STATE + 2 * LANES),
        8 * fr * size * cols + 1024 * 1024,
    )(local, gate, ecum, c, spread, prev, gain, *states)


def project_kernel(offsets, w_ref, *rest):
    count = len(offsets)
    gated, squares, (o_ref, sq_ref) = rest[:count], rest[count : 2 * count], rest[2 * count :]
    total = None
    for ref, (lo, hi) in zip(gated, offsets):
        part = dot(ref[0], w_ref[lo:hi])
        total = part if total is None else total + part
    o_ref[0] = total
    sq_ref[0] = sum(ref[0] for ref in squares)


def project(gated, squares, w_out, offsets):
    fr, npos, _ = gated[0].shape
    cols = sum(g.shape[2] for g in gated)
    return call(
        functools.partial(project_kernel, offsets),
        "project",
        (fr,),
        [full(w_out.shape)]
        + [pl.BlockSpec((1, npos, g.shape[2]), lambda f: (f, 0, 0)) for g in gated]
        + [pl.BlockSpec((1, npos, LANES), lambda f: (f, 0, 0)) for _ in squares],
        [
            pl.BlockSpec((1, npos, D), lambda f: (f, 0, 0)),
            pl.BlockSpec((1, npos, LANES), lambda f: (f, 0, 0)),
        ],
        [
            jax.ShapeDtypeStruct((fr, npos, D), F32),
            jax.ShapeDtypeStruct((fr, npos, LANES), F32),
        ],
        2 * fr * npos * cols * D,
        2 * (fr * npos * cols + cols * D) + 4 * fr * npos * D,
    )(w_out, *gated, *squares)


def last_kernel(npos, local_ref, z_ref, ecum_ref, c_ref, spread_ref, prev_ref, gain_ref, w_ref, acc_ref, sq_ref, tok_ref, *rest):
    *states, o_ref = rest
    gated = gated_of(npos, local_ref, z_ref, ecum_ref, c_ref, spread_ref, prev_ref, states)
    squares = sq_ref[0] + lane_sums(gated * gated)
    mean = jnp.sum(squares, axis=1, keepdims=True) * (1.0 / DI)
    inv_scale = lax.rsqrt(mean + 1e-05)
    total = acc_ref[0] + dot((gated * gain_ref[...]).astype(BF), w_ref[...])
    o_ref[0] = (total * inv_scale + tok_ref[0].astype(F32)).astype(BF)


def last(local, gate, ecum, c, spread, prev, gain, w_out, acc, squares, tok, states, head0):
    fr, npos, cols = local.shape
    size = c.shape[1]
    own = head0 * HEAD_DIM // cols
    per_frame = lambda f: (f, 0, 0)
    return call(
        functools.partial(last_kernel, npos),
        "last",
        (fr,),
        [
            pl.BlockSpec((1, npos, cols), per_frame),
            pl.BlockSpec((1, npos, cols), lambda f: (f, 0, own)),
            pl.BlockSpec((1, 2, size, LANES), lambda f: (f, 0, 0, 0)),
            pl.BlockSpec((1, size, STATE), per_frame),
            pl.BlockSpec((LANES, cols), lambda f: (0, own)),
            pl.BlockSpec((1, 1, cols), lambda f: (f, 0, own)),
            pl.BlockSpec((1, cols), lambda f: (0, own)),
            pl.BlockSpec((cols, D), lambda f: (own, 0)),
            pl.BlockSpec((1, npos, D), per_frame),
            pl.BlockSpec((1, npos, LANES), per_frame),
            pl.BlockSpec((1, npos, D), per_frame),
        ]
        + [pl.BlockSpec((1, STATE, cols), per_frame)] * len(states),
        pl.BlockSpec((1, npos, D), per_frame),
        jax.ShapeDtypeStruct((fr, npos, D), BF),
        2 * fr * npos * cols * D,
        8 * fr * npos * D,
    )(local, gate, ecum, c, spread, prev, gain, w_out, acc, squares, tok, *states)


def relay(end, growth):
    count = lax.axis_size("space")
    if count == 4:
        first = lax.ppermute(end, "space", [(0, 1), (2, 3)])
        joined = (end.astype(F32) + growth * first.astype(F32)).astype(BF)
        second = lax.ppermute(joined, "space", [(1, 2)])
        third = lax.ppermute(joined, "space", [(1, 3)])
        return [first, second, third]
    start = jnp.zeros_like(end)
    for _ in range(count - 1):
        moving = (end.astype(F32) + growth * start.astype(F32)).astype(BF)
        start = lax.ppermute(moving, "space", [(i, i + 1) for i in range(count - 1)])
    return [start]


def body(
    tokens, w_in, w_out, a_log_time, a_log_space, dt_bias_time, dt_bias_space, skip_time, skip_space, norm_gain
):
    fr, rows_dev, cols_dev, _ = tokens.shape
    n = lax.axis_size("tm")
    npos = rows_dev * cols_dev
    m = -(-(npos // BLK) // n)
    size = m * n * BLK
    tok = tokens.reshape(fr, npos, D)
    flat = tokens.reshape(fr * npos, D)

    tok_t = lax.all_to_all(arrange(tok, n, m), "tm", split_axis=0, concat_axis=0, tiled=True)

    base = 2 * DI
    w_small = jnp.pad(w_in[:, base:], ((0, 0), (0, 64)))
    pad = jnp.zeros((LANES - 2 * HEADS,), F32)
    bias = jnp.concatenate([dt_bias_time, dt_bias_space, pad])[None]
    rate = jnp.concatenate([-jnp.exp(a_log_time) * LOG2E, -jnp.exp(a_log_space) * LOG2E, pad])[None]
    skip_t = jnp.repeat(skip_time, HEAD_DIM)[None]
    skip_s = jnp.repeat(skip_space, HEAD_DIM)[None]
    gain = norm_gain[None]
    lane_head = jnp.arange(LANES)[:, None] - HEADS
    spread = (lane_head == jnp.arange(DI)[None, :] // HEAD_DIM).astype(BF)

    gate = gate_proj(flat, w_in).reshape(fr, npos, DI)
    score, cum, row, tail, ecum, b, c, total = space_prep(tok, w_small, bias, rate, size)
    growth = jnp.repeat(jnp.exp2(total[:, :, HEADS : 2 * HEADS]), HEAD_DIM, axis=2)
    count = lax.axis_size("space")
    prev = lax.ppermute(growth, "space", [(i, i + 1) for i in range(count - 1)])

    prep = time_prep(tok_t, w_small, bias, rate)
    starts = [sum(GROUPS[:i]) for i in range(len(GROUPS))]
    returned = []
    for head0, heads in zip(starts, GROUPS):
        out = time_scan(tok_t, w_in, prep, skip_t, head0, heads)
        returned.append(lax.all_to_all(out, "tm", split_axis=0, concat_axis=0, tiled=True))
    gated, squares, offsets = [], [], []
    for index, (head0, heads) in enumerate(zip(starts, GROUPS)):
        arrived = returned[index]
        lo, hi = head0 * HEAD_DIM, (head0 + heads) * HEAD_DIM
        states = relay(end_state(arrived, tail, b, spread, head0), growth[:, :, lo:hi])
        local = local_scan(arrived, score, cum, row, skip_s, head0, npos)
        if index < len(GROUPS) - 1:
            g, sq = finish(local, gate, ecum, c, spread, prev, gain, states, head0)
            gated.append(g)
            squares.append(sq)
            offsets.append((lo, hi))
        else:
            acc, sq = project(gated, squares, w_out, offsets)
            out = last(
                local, gate, ecum, c, spread, prev, gain, w_out, acc, sq, tok, states, head0
            )
    return out.reshape(tokens.shape)


def solution(mesh):
    placed = (P("tm", "space", None, None), P(), P(), P(), P(), P(), P(), P(), P(), P())
    return jax.shard_map(
        body, mesh=mesh, in_specs=placed, out_specs=P("tm", "space", None, None), check_vma=False
    )
```

```python
import functools

import jax
import jax.numpy as jnp
from jax import lax
from jax.experimental import pallas as pl
from jax.experimental.pallas import tpu as pltpu
from jax.sharding import PartitionSpec as P

D = 1024
HEADS = 32
HEAD_DIM = 64
STATE = 64
DI = 2048
BLK = 16
LANES = 128
LOG2E = 1.4426950408889634
TOP = 64.0
GROUPS = (16, 8, 8)
RELAY = 8
EARLY = 1
TIME_STEP = 8
BF = jnp.bfloat16
F32 = jnp.float32
VMEM = 58 * 1024 * 1024
VMEM_TAIL = 58 * 1024 * 1024


def call(kernel, name, grid, in_specs, out_specs, out_shape, flops, moved, scratch=(), vmem=VMEM):
    return pl.pallas_call(
        kernel,
        name=name,
        grid=grid,
        in_specs=in_specs,
        out_specs=out_specs,
        out_shape=out_shape,
        scratch_shapes=scratch,
        compiler_params=pltpu.CompilerParams(vmem_limit_bytes=vmem),
        cost_estimate=pl.CostEstimate(flops=flops, bytes_accessed=moved, transcendentals=0),
    )


def dot(a, b):
    return jnp.dot(a, b, preferred_element_type=F32)


def dot_nt(a, b):
    return lax.dot_general(a, b, (((1,), (1,)), ((), ())), preferred_element_type=F32)


def dot_tn(a, b):
    return lax.dot_general(a, b, (((0,), (0,)), ((), ())), preferred_element_type=F32)


def softplus(x):
    return jnp.maximum(x, 0.0) + jnp.log1p(jnp.exp(-jnp.abs(x)))


def split2(v):
    high = v.astype(BF)
    return high, (v - high.astype(F32)).astype(BF)


def spread_heads(head0, cols):
    row = lax.broadcasted_iota(jnp.int32, (LANES, cols), 0)
    col = lax.broadcasted_iota(jnp.int32, (LANES, cols), 1)
    return jnp.where(row - HEADS - head0 == col // HEAD_DIM, 1.0, 0.0).astype(BF)


def widen(values, spread):
    high, low = split2(values)
    return dot(high, spread) + dot(low, spread)


def full(shape):
    return pl.BlockSpec(shape, lambda *_: (0,) * len(shape))


def arrange_kernel(n, spare, x_ref, o_ref):
    for f in range(x_ref.shape[0]):
        o_ref[:, 0, f] = x_ref[f].reshape(n, BLK, D)
    if spare:

        @pl.when(pl.program_id(0) == pl.num_programs(0) - 1)
        def _():
            o_ref[n - spare :, 0] = jnp.zeros((spare,) + o_ref.shape[2:], BF)


def arrange(tok, n, m):
    fr, npos, _ = tok.shape
    spare = n * m - npos // BLK
    return call(
        functools.partial(arrange_kernel, n, spare),
        "arrange",
        (m,),
        [pl.BlockSpec((fr, n * BLK, D), lambda h: (0, h, 0))],
        pl.BlockSpec((n, 1, fr, BLK, D), lambda h: (0, h, 0, 0, 0)),
        jax.ShapeDtypeStruct((n, m, fr, BLK, D), BF),
        0,
        4 * fr * npos * D,
    )(tok)


def gate_kernel(x_ref, w_ref, o_ref):
    o_ref[...] = dot_nt(x_ref[...], w_ref[...]).astype(BF)


def gate_proj(flat, w_t):
    rows = flat.shape[0]
    return call(
        gate_kernel,
        "gate_proj",
        (2,),
        [full((rows, D)), pl.BlockSpec((DI // 2, D), lambda j: (j, 0))],
        pl.BlockSpec((rows, DI // 2), lambda j: (0, j)),
        jax.ShapeDtypeStruct((rows, DI), BF),
        2 * rows * D * DI,
        2 * (rows * D + D * DI + rows * DI),
    )(flat, w_t)


def small_proj(x, w_ref, raw_w_ref):
    raw = dot_nt(x, raw_w_ref[...])
    zeros = jnp.zeros((raw.shape[0], LANES - raw.shape[1]), F32)
    return dot_nt(x, w_ref[...]), jnp.concatenate([raw, zeros], axis=1)


def small_specs(group):
    first = 2 * DI // LANES + group
    raw = (2 * DI + 4 * STATE) // (2 * HEADS)
    return [
        pl.BlockSpec((LANES, D), lambda *_: (first, 0)),
        pl.BlockSpec((2 * HEADS, D), lambda *_: (raw, 0)),
    ]


def space_prep_kernel(
    npos, x_ref, w_ref, raw_w_ref, par_ref, score_ref, cum_ref, row_ref, tail_ref, ecum_ref, b_ref, c_ref, grow_ref
):
    size = score_ref.shape[1]
    bc, raw = small_proj(x_ref[0], w_ref, raw_w_ref)
    pad = jnp.zeros((size - npos, LANES), F32)
    bc = jnp.concatenate([bc.astype(BF).astype(F32), pad], axis=0)
    b = bc[:, :STATE].astype(BF)
    c = bc[:, STATE:].astype(BF)
    step = softplus(raw + par_ref[0:1])
    step = jnp.concatenate([step, pad], axis=0)
    dec = step * par_ref[1:2]
    ri = lax.broadcasted_iota(jnp.int32, (size, size), 0)
    ci = lax.broadcasted_iota(jnp.int32, (size, size), 1)
    causal = ri >= ci
    cum = jnp.dot(
        causal.astype(F32), dec, precision=lax.Precision.HIGHEST, preferred_element_type=F32
    )
    total = cum[npos - 1 : npos]
    rowterm = jnp.log2(step) - cum
    score_ref[0] = jnp.where(causal, dot_nt(c, b), 0.0)
    cum_ref[0] = cum
    row_ref[0] = rowterm.T[HEADS : 2 * HEADS]
    tail = jnp.exp2(jnp.minimum(total + rowterm, TOP))
    t_hi, t_lo = split2(tail)
    tail_ref[0, 0] = t_hi
    tail_ref[0, 1] = t_lo
    e_hi, e_lo = split2(jnp.exp2(cum))
    ecum_ref[0, 0] = e_hi
    ecum_ref[0, 1] = e_lo
    b_ref[0] = b
    c_ref[0] = c
    growth = jnp.broadcast_to(jnp.exp2(total), (8, LANES))
    grow_ref[0] = widen(growth, spread_heads(0, DI))[0:1]


def space_prep(tok, w_t, params, size):
    fr, npos, _ = tok.shape

    def per_frame(shape):
        return pl.BlockSpec((1,) + shape, lambda f: (f,) + (0,) * len(shape))

    shapes = [
        ((size, size), F32),
        ((size, LANES), F32),
        ((HEADS, size), F32),
        ((2, size, LANES), BF),
        ((2, size, LANES), BF),
        ((size, STATE), BF),
        ((size, STATE), BF),
        ((1, DI), F32),
    ]
    return call(
        functools.partial(space_prep_kernel, npos),
        "space_prep",
        (fr,),
        [per_frame((npos, D))] + small_specs(1) + [full(params.shape)],
        [per_frame(s) for s, _ in shapes],
        [jax.ShapeDtypeStruct((fr,) + s, t) for s, t in shapes],
        2 * fr * npos * D * 256,
        6 * 1024 * 1024,
    )(tok, w_t, w_t, params)


def time_prep(n, m, fr, x, w_ref, raw_w_ref, par_ref, score_ref, cum_ref, row_ref):
    bc, raw = small_proj(x, w_ref, raw_w_ref)
    shape = (n, m, fr, 2, 8, LANES)
    q_rows = n * fr * 8
    bc = bc.astype(BF).astype(F32).reshape(shape)
    step = softplus(raw.astype(BF).astype(F32) + par_ref[0:1])
    dec = (step * par_ref[1:2]).reshape(shape)
    step = step.reshape(shape)
    ri = lax.broadcasted_iota(jnp.int32, (q_rows, q_rows), 0)
    ci = lax.broadcasted_iota(jnp.int32, (q_rows, q_rows), 1)
    keep = (ri >= ci) & ((ri & 7) == (ci & 7))
    for h in range(m):
        for e in range(2):
            q = 2 * h + e
            running = jnp.zeros((8, LANES), F32)
            parts = []
            for s in range(n):
                for f in range(fr):
                    running = running + dec[s, h, f, e]
                    parts.append(running)
            cum = jnp.concatenate(parts, axis=0)
            bcq = bc[:, h, :, e].reshape(q_rows, LANES)
            b = bcq[:, :STATE].astype(BF)
            c = bcq[:, STATE:].astype(BF)
            score_ref[q] = jnp.where(keep, dot_nt(c, b), 0.0)
            cum_ref[q] = cum
            rowterm = jnp.log2(step[:, h, :, e].reshape(q_rows, LANES)) - cum
            row_ref[q] = rowterm.T[:HEADS]


def head_pair(score, cum, row, x_pair):
    rows = x_pair.shape[0]
    lane = lax.broadcasted_iota(jnp.int32, (1, LANES), 1)
    left = jnp.where(lane < HEAD_DIM, 1.0, 0.0).astype(BF)
    halves = (x_pair * left, x_pair * (1 - left))
    cols = [jnp.broadcast_to(c, (rows, LANES)) for c in cum]
    out = [None] * (rows // LANES)
    for j in range(rows // LANES):
        lo, hi = j * LANES, (j + 1) * LANES
        pieces = []
        for k in range(2):
            span = cols[k][lo:] + row[k][:, lo:hi]
            pieces.append((jnp.exp2(jnp.minimum(span, TOP)) * score[lo:, lo:hi]).astype(BF))
        keys = jnp.concatenate([halves[0][lo:hi], halves[1][lo:hi]], axis=0)
        part = dot(jnp.concatenate(pieces, axis=1), keys)
        for i in range(j, rows // LANES):
            block = part[(i - j) * LANES : (i - j + 1) * LANES]
            out[i] = block if out[i] is None else out[i] + block
    return jnp.concatenate(out, axis=0)


def head_pairs(score, cum, row_ref, row_at, head0, lane0, x):
    ys = []
    for p in range(x.shape[1] // LANES):
        pair = (2 * p, 2 * p + 1)
        ys.append(
            head_pair(
                score,
                [cum[:, lane0 + k : lane0 + k + 1] for k in pair],
                [row_ref[row_at, pl.ds(head0 + k, 1), :] for k in pair],
                x[:, p * LANES : (p + 1) * LANES],
            )
        )
    return jnp.concatenate(ys, axis=1)


def time_scan_kernel(n, m, fr, head0, first, x_ref, w_ref, *rest):
    if first:
        small, (par_ref, o_ref, score_ref, cum_ref, row_ref) = rest[:2], rest[2:]

        @pl.when(pl.program_id(0) == 0)
        def _():
            time_prep(n, m, fr, x_ref[...], *small, par_ref, score_ref, cum_ref, row_ref)

    else:
        score_ref, cum_ref, row_ref, par_ref, o_ref = rest
    q_rows = n * fr * 8
    cols = w_ref.shape[0]
    base = head0 + cols // HEAD_DIM * pl.program_id(0)
    skip = widen(par_ref[...], spread_heads(base, cols))[2:3]
    x = dot_nt(x_ref[...], w_ref[...]).astype(BF).astype(F32)
    x = x.reshape(n, m, fr, 2, 8, cols)
    for h in range(m):
        ys = []
        for e in range(2):
            q = 2 * h + e
            xq = x[:, h, :, e].reshape(q_rows, cols)
            cum = pltpu.roll(cum_ref[q], LANES - base, 1)
            y = head_pairs(score_ref.at[q], cum, row_ref, q, base, 0, xq.astype(BF))
            y = y + skip * xq
            ys.append(y.reshape(n, fr, 8, cols))
        o_ref[:, h] = jnp.concatenate(ys, axis=2).astype(BF)


def time_scan(tok_t, w_t, prep, params, head0, heads):
    n, m, fr = tok_t.shape[:3]
    rows = n * m * fr * BLK
    q_rows = n * fr * 8
    cols = heads * HEAD_DIM
    block = TIME_STEP * HEAD_DIM
    lo = (DI + head0 * HEAD_DIM) // block
    shapes = [(2 * m, q_rows, q_rows), (2 * m, q_rows, LANES), (2 * m, HEADS, q_rows)]
    prep_specs = [full(s) for s in shapes]
    out_specs = [pl.BlockSpec((n, m, fr, BLK, block), lambda j: (0, 0, 0, 0, j))]
    out_shapes = [jax.ShapeDtypeStruct((n, m, fr, BLK, cols), BF)]
    in_specs = [full((rows, D)), pl.BlockSpec((block, D), lambda j: (lo + j, 0))]
    if prep is None:
        in_specs += small_specs(0) + [full(params.shape)]
        args = (w_t, w_t, params)
        out_specs += prep_specs
        out_shapes += [jax.ShapeDtypeStruct(s, F32) for s in shapes]
    else:
        in_specs += prep_specs + [full(params.shape)]
        args = (*prep, params)
    return call(
        functools.partial(time_scan_kernel, n, m, fr, head0, prep is None),
        "time_scan",
        (cols // block,),
        in_specs,
        out_specs,
        out_shapes,
        2 * rows * D * cols + 4 * rows * q_rows * cols,
        2 * (rows * D + D * cols + rows * cols) + 2 * 1024 * 1024,
    )(tok_t.reshape(rows, D), w_t, *args)


def frame_rows(ref, frame):
    n, m, _, _, cols = ref.shape
    return jnp.concatenate([ref[:, h, frame].reshape(n * BLK, cols) for h in range(m)], axis=0)


def end_of(x, f, tail_ref, b_ref, spread):
    wide = dot(tail_ref[f, 0], spread) + dot(tail_ref[f, 1], spread)
    return dot_tn(b_ref[f], (x.astype(F32) * wide).astype(BF)).astype(BF)


def local_of(x, f, head0, score_ref, cum_ref, row_ref, skip):
    y = head_pairs(score_ref.at[f], cum_ref[f], row_ref, f, head0, HEADS + head0, x)
    return y + skip * x.astype(F32)


def space_kernel(head0, npos, local, x_ref, score_ref, cum_ref, row_ref, tail_ref, b_ref, par_ref, *outs):
    spread = spread_heads(head0, x_ref.shape[4])
    skip = widen(par_ref[...], spread)[3:4]
    for f in range(x_ref.shape[2]):
        x = frame_rows(x_ref, f)
        for i, ref in enumerate(outs[local:]):
            own = slice(i * RELAY * HEAD_DIM, i * RELAY * HEAD_DIM + ref.shape[2])
            ref[f] = end_of(x[:, own], f, tail_ref, b_ref, spread[:, own])
        if local:
            outs[0][f] = local_of(x, f, head0, score_ref, cum_ref, row_ref, skip)[:npos]


def space_parts(time_out, space, params, head0, npos, local, end):
    n, m, fr, _, cols = time_out.shape
    size = space[0].shape[1]
    step = 2 if fr % 2 == 0 else 1

    def frames(shape):
        return pl.BlockSpec((step,) + shape, lambda f: (f,) + (0,) * len(shape))

    def unused(shape):
        return pl.BlockSpec(memory_space=pl.ANY)

    l_frames = frames if local else unused
    e_frames = frames if end else unused
    outs = []
    if local:
        outs.append((frames((npos, cols)), jax.ShapeDtypeStruct((fr, npos, cols), F32)))
    if end:
        width = RELAY * HEAD_DIM
        for at in range(0, cols, width):
            piece = min(width, cols - at)
            outs.append((frames((STATE, piece)), jax.ShapeDtypeStruct((fr, STATE, piece), BF)))
    return call(
        functools.partial(space_kernel, head0, npos, local),
        "space" + "_local" * local + "_end" * end,
        (fr // step,),
        [
            pl.BlockSpec((n, m, step, BLK, cols), lambda f: (0, 0, f, 0, 0)),
            l_frames((size, size)),
            l_frames((size, LANES)),
            l_frames((HEADS, size)),
            e_frames((2, size, LANES)),
            e_frames((size, STATE)),
            full(params.shape),
        ],
        [spec for spec, _ in outs],
        [shape for _, shape in outs],
        4 * fr * size * size * cols,
        6 * fr * size * cols + 2 * 1024 * 1024,
    )(time_out, *space, params)


def gated_of(local, z, ecum_ref, c_ref, spread, states):
    state = sum(ref[0].astype(F32) for ref in states)
    npos = local.shape[0]
    carried = dot(c_ref[0], state.astype(BF))[:npos]
    wide = (dot(ecum_ref[0, 0], spread) + dot(ecum_ref[0, 1], spread))[:npos]
    z = z.astype(F32)
    return (local + wide * carried) * (z * jax.nn.sigmoid(z))


def lane_sums(v):
    return sum(v[:, a : a + LANES] for a in range(0, v.shape[1], LANES))


def finish_heads(cuts, locals_, states, z_ref, ecum_ref, c_ref, gain_ref, w_ref):
    total, squares, used = None, None, 0
    base = cuts[0][0]
    for local, (lo, hi) in zip(locals_, cuts):
        pieces = -(-(hi - lo) // (RELAY * HEAD_DIM))
        hops = len(states) // sum(-(-(b - a) // (RELAY * HEAD_DIM)) for a, b in cuts)
        for p in range(pieces):
            at, to = lo + p * RELAY * HEAD_DIM, min(hi, lo + (p + 1) * RELAY * HEAD_DIM)
            own = slice(at - base, to - base)
            gated = gated_of(
                local[0, :, at - lo : to - lo],
                z_ref[0, :, own],
                ecum_ref,
                c_ref,
                spread_heads(at // HEAD_DIM, to - at),
                states[used : used + hops],
            )
            used += hops
            part = dot((gated * gain_ref[:, own]).astype(BF), w_ref[own])
            square = lane_sums(gated * gated)
            total = part if total is None else total + part
            squares = square if squares is None else squares + square
    return total, squares


def early_kernel(cuts, z_ref, ecum_ref, c_ref, gain_ref, w_ref, *rest):
    count = len(cuts)
    locals_, states, (o_ref, sq_ref) = rest[:count], rest[count:-2], rest[-2:]
    o_ref[0], sq_ref[0] = finish_heads(cuts, locals_, states, z_ref, ecum_ref, c_ref, gain_ref, w_ref)


def last_kernel(cuts, z_ref, ecum_ref, c_ref, gain_ref, w_ref, acc_ref, sq_ref, tok_ref, *rest):
    count = len(cuts)
    locals_, states, o_ref = rest[:count], rest[count:-1], rest[-1]
    total, squares = finish_heads(cuts, locals_, states, z_ref, ecum_ref, c_ref, gain_ref, w_ref)
    mean = jnp.sum(squares + sq_ref[0], axis=1, keepdims=True) * (1.0 / DI)
    inv_scale = lax.rsqrt(mean + 1e-05)
    o_ref[0] = ((total + acc_ref[0]) * inv_scale + tok_ref[0].astype(F32)).astype(BF)


def finish(cuts, locals_, states, gate, ecum, c, gain, w_out, before=None):
    fr, npos, _ = gate.shape
    size = c.shape[1]
    cols = cuts[-1][1] - cuts[0][0]
    own = cuts[0][0] // cols
    per_frame = lambda f: (f, 0, 0)
    wide, narrow = pl.BlockSpec((1, npos, D), per_frame), pl.BlockSpec((1, npos, LANES), per_frame)
    in_specs = [
        pl.BlockSpec((1, npos, cols), lambda f: (f, 0, own)),
        pl.BlockSpec((1, 2, size, LANES), lambda f: (f, 0, 0, 0)),
        pl.BlockSpec((1, size, STATE), per_frame),
        pl.BlockSpec((1, cols), lambda f: (0, own)),
        pl.BlockSpec((cols, D), lambda f: (own, 0)),
    ]
    if before is None:
        kernel, before, name = early_kernel, (), "early"
        out_specs = [wide, narrow]
        out_shape = [
            jax.ShapeDtypeStruct((fr, npos, D), F32),
            jax.ShapeDtypeStruct((fr, npos, LANES), F32),
        ]
    else:
        kernel, name = last_kernel, "last"
        in_specs += [wide, narrow, wide]
        out_specs, out_shape = wide, jax.ShapeDtypeStruct((fr, npos, D), BF)
    return call(
        functools.partial(kernel, cuts),
        name,
        (fr,),
        in_specs + [pl.BlockSpec((1,) + v.shape[1:], per_frame) for v in (*locals_, *states)],
        out_specs,
        out_shape,
        2 * fr * npos * cols * D,
        8 * fr * npos * cols + 2 * cols * D + 4 * fr * npos * D,
        vmem=VMEM_TAIL,
    )(gate, ecum, c, gain, w_out, *before, *locals_, *states)


def hop(state, k):
    return lax.ppermute(state, "space", [(k, k + 1)])


def join(end, growth, start):
    return (end.astype(F32) + growth * start.astype(F32)).astype(BF)


def after(value, other):
    return lax.optimization_barrier((value, other))[0]


def body(
    tokens, w_in, w_out, a_log_time, a_log_space, dt_bias_time, dt_bias_space, skip_time, skip_space, norm_gain
):
    fr, rows_dev, cols_dev, _ = tokens.shape
    n = lax.axis_size("tm")
    npos = rows_dev * cols_dev
    m = -(-(npos // BLK) // n)
    size = m * n * BLK
    tok = tokens.reshape(fr, npos, D)
    flat = tokens.reshape(fr * npos, D)

    tok_t = lax.all_to_all(arrange(tok, n, m), "tm", split_axis=0, concat_axis=0, tiled=True)

    w_t = w_in.T
    fill = jnp.zeros((LANES - 2 * HEADS,), F32)
    none = jnp.zeros((HEADS,), F32)
    params = jnp.stack(
        [
            jnp.concatenate([dt_bias_time, dt_bias_space, fill]),
            jnp.concatenate([-jnp.exp(a_log_time) * LOG2E, -jnp.exp(a_log_space) * LOG2E, fill]),
            jnp.concatenate([none, skip_time, fill]),
            jnp.concatenate([none, skip_space, fill]),
        ]
        + [jnp.zeros((LANES,), F32)] * 4
    )
    gain = norm_gain[None]

    gate = gate_proj(flat, w_t).reshape(fr, npos, DI)
    score, cum, row, tail, ecum, b, c, growth = space_prep(tok, w_t, params, size)
    tok_t, gate, growth = lax.optimization_barrier((tok_t, gate, growth))

    starts = [sum(GROUPS[:i]) for i in range(len(GROUPS))]
    space = (score, cum, row, tail, b)
    prep = None
    outs = []
    for head0, heads in zip(starts, GROUPS):
        out, *made = time_scan(tok_t, w_t, prep, params, head0, heads)
        prep = prep or made
        outs.append(out)
    hops = lax.axis_size("space") - 1
    locals_, cuts, ends, grows, states = [], [], [], [], []

    def send(i, k, beside):
        moving = ends[i]
        if k:
            got = after(states[i][k - 1], beside)
            moving = [join(e, g, r) for e, g, r in zip(ends[i], grows[i], got)]
        states[i].append([hop(e, k) for e in moving])
        return moving

    for i, head0 in enumerate(starts):
        arrived = lax.all_to_all(outs[i], "tm", split_axis=0, concat_axis=0, tiled=True)
        arrived, outs[i + 1 :] = after((arrived, outs[i + 1 :]), ends[-1:])
        lo, hi = head0 * HEAD_DIM, (head0 + GROUPS[i]) * HEAD_DIM
        if i < len(GROUPS) - 1:
            local, *end = space_parts(arrived, space, params, head0, npos, True, True)
        else:
            end = space_parts(arrived, space, params, head0, npos, False, True)
            (local,) = space_parts(arrived, space, params, head0, npos, True, False)
        locals_.append(local)
        cuts.append((lo, hi))
        ends.append(end)
        width = RELAY * HEAD_DIM
        grows.append([growth[:, :, at : min(hi, at + width)] for at in range(lo, hi, width)])
        states.append([])
        send(i, 0, None)
        for j in range(i):
            if i - j <= hops - 1:
                send(j, i - j, end)
    moved = []
    for j in range(EARLY, len(GROUPS)):
        if len(states[j]) < hops:
            moved.append(send(j, len(states[j]), locals_[-1]))
    for j in range(EARLY):
        while len(states[j]) < hops:
            send(j, len(states[j]), locals_[-1])
    flat_states = lambda a, b: [r[p] for i in range(a, b) for p in range(len(ends[i])) for r in states[i]]
    acc, squares = finish(
        cuts[:EARLY], locals_[:EARLY], flat_states(0, EARLY), after(gate, moved), ecum, c, gain, w_out
    )
    for j in range(EARLY, len(GROUPS)):
        while len(states[j]) < hops:
            send(j, len(states[j]), squares)
    out = finish(
        cuts[EARLY:],
        locals_[EARLY:],
        flat_states(EARLY, len(GROUPS)),
        gate,
        ecum,
        c,
        gain,
        w_out,
        (acc, squares, tok),
    )
    return out.reshape(tokens.shape)


def solution(mesh):
    placed = (P("tm", "space", None, None), P(), P(), P(), P(), P(), P(), P(), P(), P())
    return jax.shard_map(
        body, mesh=mesh, in_specs=placed, out_specs=P("tm", "space", None, None), check_vma=False
    )
```

```python
import functools

import jax
import jax.numpy as jnp
from jax import lax
from jax.experimental import pallas as pl
from jax.experimental.pallas import tpu as pltpu
from jax.sharding import PartitionSpec as P

D = 1024
HEADS = 32
HEAD_DIM = 64
STATE = 64
DI = 2048
BLK = 16
LANES = 128
LOG2E = 1.4426950408889634
TOP = 64.0
GROUPS = (16, 8, 8)
RELAY = 16
EARLY = 1
TIME_STEP = 8
BF = jnp.bfloat16
F32 = jnp.float32
VMEM = 58 * 1024 * 1024
VMEM_TAIL = 40 * 1024 * 1024


def call(kernel, name, grid, in_specs, out_specs, out_shape, flops, moved, scratch=(), vmem=VMEM):
    return pl.pallas_call(
        kernel,
        name=name,
        grid=grid,
        in_specs=in_specs,
        out_specs=out_specs,
        out_shape=out_shape,
        scratch_shapes=scratch,
        compiler_params=pltpu.CompilerParams(vmem_limit_bytes=vmem),
        cost_estimate=pl.CostEstimate(flops=flops, bytes_accessed=moved, transcendentals=0),
    )


def dot(a, b):
    return jnp.dot(a, b, preferred_element_type=F32)


def dot_nt(a, b):
    return lax.dot_general(a, b, (((1,), (1,)), ((), ())), preferred_element_type=F32)


def dot_tn(a, b):
    return lax.dot_general(a, b, (((0,), (0,)), ((), ())), preferred_element_type=F32)


def softplus(x):
    return jnp.maximum(x, 0.0) + jnp.log1p(jnp.exp(-jnp.abs(x)))


def spread_heads(head0, cols):
    row = lax.broadcasted_iota(jnp.int32, (LANES, cols), 0)
    col = lax.broadcasted_iota(jnp.int32, (LANES, cols), 1)
    return jnp.where(row - HEADS - head0 == col // HEAD_DIM, 1.0, 0.0).astype(BF)


def split2(v):
    high = v.astype(BF)
    return jnp.concatenate([high, (v - high.astype(F32)).astype(BF)], axis=1)


def widen_split(parts, spread):
    return dot(parts, jnp.concatenate([spread, spread], axis=0))


def widen(values, spread):
    return widen_split(split2(values), spread)


def full(shape):
    return pl.BlockSpec(shape, lambda *_: (0,) * len(shape))


def arrange_kernel(n, spare, x_ref, o_ref):
    for f in range(x_ref.shape[0]):
        o_ref[:, 0, f] = x_ref[f].reshape(n, BLK, D)
    if spare:

        @pl.when(pl.program_id(0) == pl.num_programs(0) - 1)
        def _():
            o_ref[n - spare :, 0] = jnp.zeros((spare,) + o_ref.shape[2:], BF)


def arrange(tok, n, m):
    fr, npos, _ = tok.shape
    spare = n * m - npos // BLK
    return call(
        functools.partial(arrange_kernel, n, spare),
        "arrange",
        (m,),
        [pl.BlockSpec((fr, n * BLK, D), lambda h: (0, h, 0))],
        pl.BlockSpec((n, 1, fr, BLK, D), lambda h: (0, h, 0, 0, 0)),
        jax.ShapeDtypeStruct((n, m, fr, BLK, D), BF),
        0,
        4 * fr * npos * D,
    )(tok)


def gate_kernel(x_ref, w_ref, o_ref):
    o_ref[...] = dot_nt(x_ref[...], w_ref[...]).astype(BF)


def gate_proj(flat, w_t):
    rows = flat.shape[0]
    return call(
        gate_kernel,
        "gate_proj",
        (2,),
        [full((rows, D)), pl.BlockSpec((DI // 2, D), lambda j: (j, 0))],
        pl.BlockSpec((rows, DI // 2), lambda j: (0, j)),
        jax.ShapeDtypeStruct((rows, DI), BF),
        2 * rows * D * DI,
        2 * (rows * D + D * DI + rows * DI),
    )(flat, w_t)


def small_proj(x, w_ref, raw_w_ref):
    raw = dot_nt(x, raw_w_ref[...])
    zeros = jnp.zeros((raw.shape[0], LANES - raw.shape[1]), F32)
    return dot_nt(x, w_ref[...]), jnp.concatenate([raw, zeros], axis=1)


def small_specs(group):
    first = 2 * DI // LANES + group
    raw = (2 * DI + 4 * STATE) // (2 * HEADS)
    return [
        pl.BlockSpec((LANES, D), lambda *_: (first, 0)),
        pl.BlockSpec((2 * HEADS, D), lambda *_: (raw, 0)),
    ]


def space_prep_kernel(
    npos, x_ref, w_ref, raw_w_ref, par_ref, score_ref, cum_ref, row_ref, tail_ref, ecum_ref, b_ref, c_ref, grow_ref
):
    size = score_ref.shape[1]
    bc, raw = small_proj(x_ref[0], w_ref, raw_w_ref)
    pad = jnp.zeros((size - npos, LANES), F32)
    bc = jnp.concatenate([bc.astype(BF).astype(F32), pad], axis=0)
    b = bc[:, :STATE].astype(BF)
    c = bc[:, STATE:].astype(BF)
    step = softplus(raw + par_ref[0:1])
    step = jnp.concatenate([step, pad], axis=0)
    dec = step * par_ref[1:2]
    ri = lax.broadcasted_iota(jnp.int32, (size, size), 0)
    ci = lax.broadcasted_iota(jnp.int32, (size, size), 1)
    causal = ri >= ci
    cum = jnp.dot(
        causal.astype(F32), dec, precision=lax.Precision.HIGHEST, preferred_element_type=F32
    )
    total = cum[npos - 1 : npos]
    rowterm = jnp.log2(step) - cum
    score_ref[0] = jnp.where(causal, dot_nt(c, b), 0.0)
    cum_ref[0] = cum
    row_ref[0] = rowterm.T[HEADS : 2 * HEADS]
    tail = jnp.exp2(jnp.minimum(total + rowterm, TOP))
    tail_ref[0] = split2(tail)
    ecum_ref[0] = split2(jnp.exp2(cum))
    b_ref[0] = b
    c_ref[0] = c
    growth = jnp.broadcast_to(jnp.exp2(total), (8, LANES))
    grow_ref[0] = widen(growth, spread_heads(0, DI))[0:1]


def space_prep(tok, w_t, params, size):
    fr, npos, _ = tok.shape

    def per_frame(shape):
        return pl.BlockSpec((1,) + shape, lambda f: (f,) + (0,) * len(shape))

    shapes = [
        ((size, size), F32),
        ((size, LANES), F32),
        ((HEADS, size), F32),
        ((size, 2 * LANES), BF),
        ((size, 2 * LANES), BF),
        ((size, STATE), BF),
        ((size, STATE), BF),
        ((1, DI), F32),
    ]
    return call(
        functools.partial(space_prep_kernel, npos),
        "space_prep",
        (fr,),
        [per_frame((npos, D))] + small_specs(1) + [full(params.shape)],
        [per_frame(s) for s, _ in shapes],
        [jax.ShapeDtypeStruct((fr,) + s, t) for s, t in shapes],
        2 * fr * npos * D * 256,
        6 * 1024 * 1024,
    )(tok, w_t, w_t, params)


def time_prep(n, m, fr, x, w_ref, raw_w_ref, par_ref, score_ref, cum_ref, row_ref):
    bc, raw = small_proj(x, w_ref, raw_w_ref)
    shape = (n, m, fr, 2, 8, LANES)
    q_rows = n * fr * 8
    bc = bc.astype(BF).astype(F32).reshape(shape)
    step = softplus(raw.astype(BF).astype(F32) + par_ref[0:1])
    dec = (step * par_ref[1:2]).reshape(shape)
    step = step.reshape(shape)
    ri = lax.broadcasted_iota(jnp.int32, (q_rows, q_rows), 0)
    ci = lax.broadcasted_iota(jnp.int32, (q_rows, q_rows), 1)
    keep = (ri >= ci) & ((ri & 7) == (ci & 7))
    for h in range(m):
        for e in range(2):
            q = 2 * h + e
            running = jnp.zeros((8, LANES), F32)
            parts = []
            for s in range(n):
                for f in range(fr):
                    running = running + dec[s, h, f, e]
                    parts.append(running)
            cum = jnp.concatenate(parts, axis=0)
            bcq = bc[:, h, :, e].reshape(q_rows, LANES)
            b = bcq[:, :STATE].astype(BF)
            c = bcq[:, STATE:].astype(BF)
            score_ref[q] = jnp.where(keep, dot_nt(c, b), 0.0)
            cum_ref[q] = cum
            rowterm = jnp.log2(step[:, h, :, e].reshape(q_rows, LANES)) - cum
            row_ref[q] = rowterm.T[:HEADS]


def head_pair(score, cum, row, x_pair):
    rows = x_pair.shape[0]
    lane = lax.broadcasted_iota(jnp.int32, (1, LANES), 1)
    left = jnp.where(lane < HEAD_DIM, 1.0, 0.0).astype(BF)
    halves = (x_pair * left, x_pair * (1 - left))
    cols = [jnp.broadcast_to(c, (rows, LANES)) for c in cum]
    out = [None] * (rows // LANES)
    for j in range(rows // LANES):
        lo, hi = j * LANES, (j + 1) * LANES
        pieces = []
        for k in range(2):
            span = cols[k][lo:] + row[k][:, lo:hi]
            pieces.append((jnp.exp2(jnp.minimum(span, TOP)) * score[lo:, lo:hi]).astype(BF))
        keys = jnp.concatenate([halves[0][lo:hi], halves[1][lo:hi]], axis=0)
        part = dot(jnp.concatenate(pieces, axis=1), keys)
        for i in range(j, rows // LANES):
            block = part[(i - j) * LANES : (i - j + 1) * LANES]
            out[i] = block if out[i] is None else out[i] + block
    return jnp.concatenate(out, axis=0)


def head_pairs(score, cum, row_ref, row_at, head0, lane0, x):
    ys = []
    for p in range(x.shape[1] // LANES):
        pair = (2 * p, 2 * p + 1)
        ys.append(
            head_pair(
                score,
                [cum[:, lane0 + k : lane0 + k + 1] for k in pair],
                [row_ref[row_at, pl.ds(head0 + k, 1), :] for k in pair],
                x[:, p * LANES : (p + 1) * LANES],
            )
        )
    return jnp.concatenate(ys, axis=1)


def time_scan_kernel(n, m, fr, head0, first, x_ref, w_ref, *rest):
    if first:
        small, (par_ref, o_ref, score_ref, cum_ref, row_ref) = rest[:2], rest[2:]

        @pl.when(pl.program_id(0) == 0)
        def _():
            time_prep(n, m, fr, x_ref[...], *small, par_ref, score_ref, cum_ref, row_ref)

    else:
        score_ref, cum_ref, row_ref, par_ref, o_ref = rest
    q_rows = n * fr * 8
    cols = w_ref.shape[0]
    base = head0 + cols // HEAD_DIM * pl.program_id(0)
    skip = widen(par_ref[...], spread_heads(base, cols))[2:3]
    x = dot_nt(x_ref[...], w_ref[...]).astype(BF).astype(F32)
    x = x.reshape(n, m, fr, 2, 8, cols)
    for h in range(m):
        ys = []
        for e in range(2):
            q = 2 * h + e
            xq = x[:, h, :, e].reshape(q_rows, cols)
            cum = pltpu.roll(cum_ref[q], LANES - base, 1)
            y = head_pairs(score_ref.at[q], cum, row_ref, q, base, 0, xq.astype(BF))
            y = y + skip * xq
            ys.append(y.reshape(n, fr, 8, cols))
        o_ref[:, h] = jnp.concatenate(ys, axis=2).astype(BF)


def time_scan(tok_t, w_t, prep, params, head0, heads):
    n, m, fr = tok_t.shape[:3]
    rows = n * m * fr * BLK
    q_rows = n * fr * 8
    cols = heads * HEAD_DIM
    block = TIME_STEP * HEAD_DIM
    lo = (DI + head0 * HEAD_DIM) // block
    shapes = [(2 * m, q_rows, q_rows), (2 * m, q_rows, LANES), (2 * m, HEADS, q_rows)]
    prep_specs = [full(s) for s in shapes]
    out_specs = [pl.BlockSpec((n, m, fr, BLK, block), lambda j: (0, 0, 0, 0, j))]
    out_shapes = [jax.ShapeDtypeStruct((n, m, fr, BLK, cols), BF)]
    in_specs = [full((rows, D)), pl.BlockSpec((block, D), lambda j: (lo + j, 0))]
    if prep is None:
        in_specs += small_specs(0) + [full(params.shape)]
        args = (w_t, w_t, params)
        out_specs += prep_specs
        out_shapes += [jax.ShapeDtypeStruct(s, F32) for s in shapes]
    else:
        in_specs += prep_specs + [full(params.shape)]
        args = (*prep, params)
    return call(
        functools.partial(time_scan_kernel, n, m, fr, head0, prep is None),
        "time_scan",
        (cols // block,),
        in_specs,
        out_specs,
        out_shapes,
        2 * rows * D * cols + 4 * rows * q_rows * cols,
        2 * (rows * D + D * cols + rows * cols) + 2 * 1024 * 1024,
    )(tok_t.reshape(rows, D), w_t, *args)


def frame_rows(ref, frame):
    n, m, _, _, cols = ref.shape
    return jnp.concatenate([ref[:, h, frame].reshape(n * BLK, cols) for h in range(m)], axis=0)


def end_of(x, f, tail_ref, b_ref, spread):
    wide = widen_split(tail_ref[f], spread)
    return dot_tn(b_ref[f], (x.astype(F32) * wide).astype(BF)).astype(BF)


def local_of(x, f, head0, score_ref, cum_ref, row_ref, skip):
    y = head_pairs(score_ref.at[f], cum_ref[f], row_ref, f, head0, HEADS + head0, x)
    return y + skip * x.astype(F32)


def space_kernel(head0, npos, local, x_ref, score_ref, cum_ref, row_ref, tail_ref, b_ref, par_ref, *outs):
    spread = spread_heads(head0, x_ref.shape[4])
    skip = widen(par_ref[...], spread)[3:4]
    for f in range(x_ref.shape[2]):
        x = frame_rows(x_ref, f)
        for i, ref in enumerate(outs[local:]):
            own = slice(i * RELAY * HEAD_DIM, i * RELAY * HEAD_DIM + ref.shape[2])
            ref[f] = end_of(x[:, own], f, tail_ref, b_ref, spread[:, own])
        if local:
            outs[0][f] = local_of(x, f, head0, score_ref, cum_ref, row_ref, skip)[:npos]


def space_parts(time_out, space, params, head0, npos, local, end):
    n, m, fr, _, cols = time_out.shape
    size = space[0].shape[1]
    step = 2 if fr % 2 == 0 else 1

    def frames(shape):
        return pl.BlockSpec((step,) + shape, lambda f: (f,) + (0,) * len(shape))

    def unused(shape):
        return pl.BlockSpec(memory_space=pl.ANY)

    l_frames = frames if local else unused
    e_frames = frames if end else unused
    outs = []
    if local:
        outs.append((frames((npos, cols)), jax.ShapeDtypeStruct((fr, npos, cols), F32)))
    if end:
        width = RELAY * HEAD_DIM
        for at in range(0, cols, width):
            piece = min(width, cols - at)
            outs.append((frames((STATE, piece)), jax.ShapeDtypeStruct((fr, STATE, piece), BF)))
    return call(
        functools.partial(space_kernel, head0, npos, local),
        "space" + "_local" * local + "_end" * end,
        (fr // step,),
        [
            pl.BlockSpec((n, m, step, BLK, cols), lambda f: (0, 0, f, 0, 0)),
            l_frames((size, size)),
            l_frames((size, LANES)),
            l_frames((HEADS, size)),
            e_frames((size, 2 * LANES)),
            e_frames((size, STATE)),
            full(params.shape),
        ],
        [spec for spec, _ in outs],
        [shape for _, shape in outs],
        4 * fr * size * size * cols,
        6 * fr * size * cols + 2 * 1024 * 1024,
    )(time_out, *space, params)


def gated_of(local, z, ecum_ref, c_ref, spread, states):
    state = sum(ref[0].astype(F32) for ref in states)
    npos = local.shape[0]
    carried = dot(c_ref[0], state.astype(BF))[:npos]
    wide = widen_split(ecum_ref[0], spread)[:npos]
    z = z.astype(F32)
    return (local + wide * carried) * (0.5 * z * (1.0 + jnp.tanh(0.5 * z)))


def lane_sums(v):
    return sum(v[:, a : a + LANES] for a in range(0, v.shape[1], LANES))


def finish_heads(cuts, locals_, states, z_ref, ecum_ref, c_ref, gain_ref, w_ref):
    total, squares, used = None, None, 0
    base = cuts[0][0]
    for local, (lo, hi) in zip(locals_, cuts):
        pieces = -(-(hi - lo) // (RELAY * HEAD_DIM))
        hops = len(states) // sum(-(-(b - a) // (RELAY * HEAD_DIM)) for a, b in cuts)
        for p in range(pieces):
            at, to = lo + p * RELAY * HEAD_DIM, min(hi, lo + (p + 1) * RELAY * HEAD_DIM)
            own = slice(at - base, to - base)
            gated = gated_of(
                local[0, :, at - lo : to - lo],
                z_ref[0, :, own],
                ecum_ref,
                c_ref,
                spread_heads(at // HEAD_DIM, to - at),
                states[used : used + hops],
            )
            used += hops
            part = dot((gated * gain_ref[:, own]).astype(BF), w_ref[own])
            square = lane_sums(gated * gated)
            total = part if total is None else total + part
            squares = square if squares is None else squares + square
    return total, squares


def early_kernel(cuts, z_ref, ecum_ref, c_ref, gain_ref, w_ref, *rest):
    count = len(cuts)
    locals_, states, (o_ref, sq_ref) = rest[:count], rest[count:-2], rest[-2:]
    o_ref[0], sq_ref[0] = finish_heads(cuts, locals_, states, z_ref, ecum_ref, c_ref, gain_ref, w_ref)


def last_kernel(cuts, z_ref, ecum_ref, c_ref, gain_ref, w_ref, acc_ref, sq_ref, tok_ref, *rest):
    count = len(cuts)
    locals_, states, o_ref = rest[:count], rest[count:-1], rest[-1]
    total, squares = finish_heads(cuts, locals_, states, z_ref, ecum_ref, c_ref, gain_ref, w_ref)
    mean = jnp.sum(squares + sq_ref[0], axis=1, keepdims=True) * (1.0 / DI)
    inv_scale = lax.rsqrt(mean + 1e-05)
    o_ref[0] = ((total + acc_ref[0]) * inv_scale + tok_ref[0].astype(F32)).astype(BF)


def finish(cuts, locals_, states, gate, ecum, c, gain, w_out, before=None):
    fr, npos, _ = gate.shape
    size = c.shape[1]
    cols = cuts[-1][1] - cuts[0][0]
    own = cuts[0][0] // cols
    per_frame = lambda f: (f, 0, 0)
    wide, narrow = pl.BlockSpec((1, npos, D), per_frame), pl.BlockSpec((1, npos, LANES), per_frame)
    in_specs = [
        pl.BlockSpec((1, npos, cols), lambda f: (f, 0, own)),
        pl.BlockSpec((1, size, 2 * LANES), per_frame),
        pl.BlockSpec((1, size, STATE), per_frame),
        pl.BlockSpec((1, cols), lambda f: (0, own)),
        pl.BlockSpec((cols, D), lambda f: (own, 0)),
    ]
    if before is None:
        kernel, before, name = early_kernel, (), "early"
        out_specs = [wide, narrow]
        out_shape = [
            jax.ShapeDtypeStruct((fr, npos, D), F32),
            jax.ShapeDtypeStruct((fr, npos, LANES), F32),
        ]
    else:
        kernel, name = last_kernel, "last"
        in_specs += [wide, narrow, wide]
        out_specs, out_shape = wide, jax.ShapeDtypeStruct((fr, npos, D), BF)
    return call(
        functools.partial(kernel, cuts),
        name,
        (fr,),
        in_specs + [pl.BlockSpec((1,) + v.shape[1:], per_frame) for v in (*locals_, *states)],
        out_specs,
        out_shape,
        2 * fr * npos * cols * D,
        8 * fr * npos * cols + 2 * cols * D + 4 * fr * npos * D,
        vmem=VMEM_TAIL,
    )(gate, ecum, c, gain, w_out, *before, *locals_, *states)


def hop(state, k):
    return lax.ppermute(state, "space", [(k, k + 1)])


def join(end, growth, start):
    return (end.astype(F32) + growth * start.astype(F32)).astype(BF)


def after(value, other):
    return lax.optimization_barrier((value, other))[0]


def body(
    tokens, w_in, w_out, a_log_time, a_log_space, dt_bias_time, dt_bias_space, skip_time, skip_space, norm_gain
):
    fr, rows_dev, cols_dev, _ = tokens.shape
    n = lax.axis_size("tm")
    npos = rows_dev * cols_dev
    m = -(-(npos // BLK) // n)
    size = m * n * BLK
    tok = tokens.reshape(fr, npos, D)
    flat = tokens.reshape(fr * npos, D)

    tok_t = lax.all_to_all(arrange(tok, n, m), "tm", split_axis=0, concat_axis=0, tiled=True)

    w_t = w_in.T
    fill = jnp.zeros((LANES - 2 * HEADS,), F32)
    none = jnp.zeros((HEADS,), F32)
    params = jnp.stack(
        [
            jnp.concatenate([dt_bias_time, dt_bias_space, fill]),
            jnp.concatenate([-jnp.exp(a_log_time) * LOG2E, -jnp.exp(a_log_space) * LOG2E, fill]),
            jnp.concatenate([none, skip_time, fill]),
            jnp.concatenate([none, skip_space, fill]),
        ]
        + [jnp.zeros((LANES,), F32)] * 4
    )
    gain = norm_gain[None]

    gate = gate_proj(flat, w_t).reshape(fr, npos, DI)
    score, cum, row, tail, ecum, b, c, growth = space_prep(tok, w_t, params, size)
    tok_t, gate, growth = lax.optimization_barrier((tok_t, gate, growth))

    starts = [sum(GROUPS[:i]) for i in range(len(GROUPS))]
    space = (score, cum, row, tail, b)
    prep = None
    outs = []
    for head0, heads in zip(starts, GROUPS):
        out, *made = time_scan(tok_t, w_t, prep, params, head0, heads)
        prep = prep or made
        outs.append(out)
    hops = lax.axis_size("space") - 1
    locals_, cuts, ends, grows, states = [], [], [], [], []

    def send(i, k, beside):
        moving = ends[i]
        if k:
            got = after(states[i][k - 1], beside)
            moving = [join(e, g, r) for e, g, r in zip(ends[i], grows[i], got)]
        states[i].append([hop(e, k) for e in moving])
        return moving

    for i, head0 in enumerate(starts):
        arrived = lax.all_to_all(outs[i], "tm", split_axis=0, concat_axis=0, tiled=True)
        arrived, outs[i + 1 :] = after((arrived, outs[i + 1 :]), ends[-1:])
        lo, hi = head0 * HEAD_DIM, (head0 + GROUPS[i]) * HEAD_DIM
        local, *end = space_parts(arrived, space, params, head0, npos, True, True)
        locals_.append(local)
        cuts.append((lo, hi))
        ends.append(end)
        width = RELAY * HEAD_DIM
        grows.append([growth[:, :, at : min(hi, at + width)] for at in range(lo, hi, width)])
        states.append([])
        moved = send(i, 0, None)
        for j in range(i):
            if i - j <= hops - 1:
                moved = moved + send(j, i - j, end)
    while any(len(hopped) < hops for hopped in states):
        for j, hopped in enumerate(states):
            if len(hopped) < hops:
                moved = send(j, len(hopped), None)
    flat_states = lambda a, b: [r[p] for i in range(a, b) for p in range(len(ends[i])) for r in states[i]]
    acc, squares = finish(
        cuts[:EARLY], locals_[:EARLY], flat_states(0, EARLY), after(gate, moved), ecum, c, gain, w_out
    )
    out = finish(
        cuts[EARLY:],
        locals_[EARLY:],
        flat_states(EARLY, len(GROUPS)),
        gate,
        ecum,
        c,
        gain,
        w_out,
        (acc, squares, tok),
    )
    return out.reshape(tokens.shape)


def solution(mesh):
    placed = (P("tm", "space", None, None), P(), P(), P(), P(), P(), P(), P(), P(), P())
    return jax.shard_map(
        body, mesh=mesh, in_specs=placed, out_specs=P("tm", "space", None, None), check_vma=False
    )
```

```python
import functools

import jax
import jax.numpy as jnp
from jax import lax
from jax.experimental import pallas as pl
from jax.experimental.pallas import tpu as pltpu
from jax.sharding import PartitionSpec as P

D = 1024
HEADS = 32
HEAD_DIM = 64
STATE = 64
DI = 2048
BLK = 16
LANES = 128
LOG2E = 1.4426950408889634
TOP = 64.0
GROUPS = (16, 8, 8)
RELAY = 16
EARLY = 1
TIME_STEP = 8
BF = jnp.bfloat16
F32 = jnp.float32
VMEM = 58 * 1024 * 1024
VMEM_TAIL = 40 * 1024 * 1024


def call(kernel, name, grid, in_specs, out_specs, out_shape, flops, moved, scratch=(), vmem=VMEM):
    return pl.pallas_call(
        kernel,
        name=name,
        grid=grid,
        in_specs=in_specs,
        out_specs=out_specs,
        out_shape=out_shape,
        scratch_shapes=scratch,
        compiler_params=pltpu.CompilerParams(vmem_limit_bytes=vmem),
        cost_estimate=pl.CostEstimate(flops=flops, bytes_accessed=moved, transcendentals=0),
    )


def dot(a, b):
    return jnp.dot(a, b, preferred_element_type=F32)


def dot_nt(a, b):
    return lax.dot_general(a, b, (((1,), (1,)), ((), ())), preferred_element_type=F32)


def dot_tn(a, b):
    return lax.dot_general(a, b, (((0,), (0,)), ((), ())), preferred_element_type=F32)


def softplus(x):
    return jnp.maximum(x, 0.0) + jnp.log1p(jnp.exp(-jnp.abs(x)))


def spread_heads(head0, cols):
    row = lax.broadcasted_iota(jnp.int32, (LANES, cols), 0)
    col = lax.broadcasted_iota(jnp.int32, (LANES, cols), 1)
    return jnp.where(row - HEADS - head0 == col // HEAD_DIM, 1.0, 0.0).astype(BF)


def split2(v):
    high = v.astype(BF)
    return jnp.concatenate([high, (v - high.astype(F32)).astype(BF)], axis=1)


def widen_split(parts, spread):
    return dot(parts, jnp.concatenate([spread, spread], axis=0))


def widen(values, spread):
    return widen_split(split2(values), spread)


def full(shape):
    return pl.BlockSpec(shape, lambda *_: (0,) * len(shape))


def arrange_kernel(n, spare, x_ref, *outs):
    last = pl.program_id(0) == pl.num_programs(0) - 1
    for k, o_ref in enumerate(outs):
        to = jnp.bitwise_xor(lax.axis_index("tm"), k)
        o_ref[0] = x_ref[:, pl.ds(pl.multiple_of(to * BLK, BLK), BLK), :]

        @pl.when(last & (to >= n - spare))
        def _():
            o_ref[0] = jnp.zeros(o_ref.shape[1:], BF)


def arrange(tok, n, m):
    fr, npos, _ = tok.shape
    spare = n * m - npos // BLK
    return call(
        functools.partial(arrange_kernel, n, spare),
        "arrange",
        (m,),
        [pl.BlockSpec((fr, n * BLK, D), lambda h: (0, h, 0))],
        [pl.BlockSpec((1, fr, BLK, D), lambda h: (h, 0, 0, 0))] * n,
        [jax.ShapeDtypeStruct((m, fr, BLK, D), BF)] * n,
        0,
        4 * fr * npos * D,
    )(tok)


def exchange(pieces):
    n = len(pieces)
    order = [k for k in range(n - 1, 1, -1)] + [1]
    got = {k: lax.ppermute(pieces[k], "tm", [(i, i ^ k) for i in range(n)]) for k in order}
    return [pieces[0]] + [got[k] for k in range(1, n)]


def gate_kernel(x_ref, w_ref, o_ref):
    o_ref[...] = dot_nt(x_ref[...], w_ref[...]).astype(BF)


def gate_proj(flat, w_t):
    rows = flat.shape[0]
    return call(
        gate_kernel,
        "gate_proj",
        (2,),
        [full((rows, D)), pl.BlockSpec((DI // 2, D), lambda j: (j, 0))],
        pl.BlockSpec((rows, DI // 2), lambda j: (0, j)),
        jax.ShapeDtypeStruct((rows, DI), BF),
        2 * rows * D * DI,
        2 * (rows * D + D * DI + rows * DI),
    )(flat, w_t)


def small_proj(x, w_ref, raw_w_ref):
    raw = dot_nt(x, raw_w_ref[...])
    zeros = jnp.zeros((raw.shape[0], LANES - raw.shape[1]), F32)
    return dot_nt(x, w_ref[...]), jnp.concatenate([raw, zeros], axis=1)


def small_specs(group):
    first = 2 * DI // LANES + group
    raw = (2 * DI + 4 * STATE) // (2 * HEADS)
    return [
        pl.BlockSpec((LANES, D), lambda *_: (first, 0)),
        pl.BlockSpec((2 * HEADS, D), lambda *_: (raw, 0)),
    ]


def space_prep_kernel(
    npos, x_ref, w_ref, raw_w_ref, par_ref, score_ref, cum_ref, row_ref, tail_ref, ecum_ref, b_ref, c_ref, grow_ref
):
    size = score_ref.shape[1]
    bc, raw = small_proj(x_ref[0], w_ref, raw_w_ref)
    pad = jnp.zeros((size - npos, LANES), F32)
    bc = jnp.concatenate([bc.astype(BF).astype(F32), pad], axis=0)
    b = bc[:, :STATE].astype(BF)
    c = bc[:, STATE:].astype(BF)
    step = softplus(raw + par_ref[0:1])
    step = jnp.concatenate([step, pad], axis=0)
    dec = step * par_ref[1:2]
    ri = lax.broadcasted_iota(jnp.int32, (size, size), 0)
    ci = lax.broadcasted_iota(jnp.int32, (size, size), 1)
    causal = ri >= ci
    cum = jnp.dot(
        causal.astype(F32), dec, precision=lax.Precision.HIGHEST, preferred_element_type=F32
    )
    total = cum[npos - 1 : npos]
    rowterm = jnp.log2(step) - cum
    score_ref[0] = jnp.where(causal, dot_nt(c, b), 0.0)
    cum_ref[0] = cum
    row_ref[0] = rowterm.T[HEADS : 2 * HEADS]
    tail = jnp.exp2(jnp.minimum(total + rowterm, TOP))
    tail_ref[0] = split2(tail)
    ecum_ref[0] = split2(jnp.exp2(cum))
    b_ref[0] = b
    c_ref[0] = c
    growth = jnp.broadcast_to(jnp.exp2(total), (8, LANES))
    grow_ref[0] = widen(growth, spread_heads(0, DI))[0:1]


def space_prep(tok, w_t, params, size):
    fr, npos, _ = tok.shape

    def per_frame(shape):
        return pl.BlockSpec((1,) + shape, lambda f: (f,) + (0,) * len(shape))

    shapes = [
        ((size, size), F32),
        ((size, LANES), F32),
        ((HEADS, size), F32),
        ((size, 2 * LANES), BF),
        ((size, 2 * LANES), BF),
        ((size, STATE), BF),
        ((size, STATE), BF),
        ((1, DI), F32),
    ]
    return call(
        functools.partial(space_prep_kernel, npos),
        "space_prep",
        (fr,),
        [per_frame((npos, D))] + small_specs(1) + [full(params.shape)],
        [per_frame(s) for s, _ in shapes],
        [jax.ShapeDtypeStruct((fr,) + s, t) for s, t in shapes],
        2 * fr * npos * D * 256,
        6 * 1024 * 1024,
    )(tok, w_t, w_t, params)


def time_prep(n, m, fr, x, w_ref, raw_w_ref, par_ref, score_ref, cum_ref, row_ref):
    bc, raw = small_proj(x, w_ref, raw_w_ref)
    shape = (n, m, fr, 2, 8, LANES)
    q_rows = n * fr * 8
    bc = bc.astype(BF).astype(F32).reshape(shape)
    step = softplus(raw.astype(BF).astype(F32) + par_ref[0:1])
    dec = (step * par_ref[1:2]).reshape(shape)
    step = step.reshape(shape)
    ri = lax.broadcasted_iota(jnp.int32, (q_rows, q_rows), 0)
    ci = lax.broadcasted_iota(jnp.int32, (q_rows, q_rows), 1)
    keep = (ri >= ci) & ((ri & 7) == (ci & 7))
    for h in range(m):
        for e in range(2):
            q = 2 * h + e
            running = jnp.zeros((8, LANES), F32)
            parts = []
            for s in range(n):
                for f in range(fr):
                    running = running + dec[s, h, f, e]
                    parts.append(running)
            cum = jnp.concatenate(parts, axis=0)
            bcq = bc[:, h, :, e].reshape(q_rows, LANES)
            b = bcq[:, :STATE].astype(BF)
            c = bcq[:, STATE:].astype(BF)
            score_ref[q] = jnp.where(keep, dot_nt(c, b), 0.0)
            cum_ref[q] = cum
            rowterm = jnp.log2(step[:, h, :, e].reshape(q_rows, LANES)) - cum
            row_ref[q] = rowterm.T[:HEADS]


def head_pair(score, cum, row, x_pair):
    rows = x_pair.shape[0]
    lane = lax.broadcasted_iota(jnp.int32, (1, LANES), 1)
    left = jnp.where(lane < HEAD_DIM, 1.0, 0.0).astype(BF)
    halves = (x_pair * left, x_pair * (1 - left))
    cols = [jnp.broadcast_to(c, (rows, LANES)) for c in cum]
    out = [None] * (rows // LANES)
    for j in range(rows // LANES):
        lo, hi = j * LANES, (j + 1) * LANES
        pieces = []
        for k in range(2):
            span = cols[k][lo:] + row[k][:, lo:hi]
            pieces.append((jnp.exp2(jnp.minimum(span, TOP)) * score[lo:, lo:hi]).astype(BF))
        keys = jnp.concatenate([halves[0][lo:hi], halves[1][lo:hi]], axis=0)
        part = dot(jnp.concatenate(pieces, axis=1), keys)
        for i in range(j, rows // LANES):
            block = part[(i - j) * LANES : (i - j + 1) * LANES]
            out[i] = block if out[i] is None else out[i] + block
    return jnp.concatenate(out, axis=0)


def head_pairs(score, cum, row_ref, row_at, head0, lane0, x):
    ys = []
    for p in range(x.shape[1] // LANES):
        pair = (2 * p, 2 * p + 1)
        ys.append(
            head_pair(
                score,
                [cum[:, lane0 + k : lane0 + k + 1] for k in pair],
                [row_ref[row_at, pl.ds(head0 + k, 1), :] for k in pair],
                x[:, p * LANES : (p + 1) * LANES],
            )
        )
    return jnp.concatenate(ys, axis=1)


def time_scan_kernel(n, m, fr, head0, first, *refs):
    pieces, w_ref, rest, x_ref = refs[:n], refs[n], refs[n + 1 : -1], refs[-1]

    @pl.when(pl.program_id(0) == 0)
    def _():
        per = m * fr * BLK
        for k, ref in enumerate(pieces):
            source = jnp.bitwise_xor(lax.axis_index("tm"), k)
            x_ref[pl.ds(pl.multiple_of(source * per, per), per), :] = ref[...]

    if first:
        small, (par_ref, o_ref, score_ref, cum_ref, row_ref) = rest[:2], rest[2:]

        @pl.when(pl.program_id(0) == 0)
        def _():
            time_prep(n, m, fr, x_ref[...], *small, par_ref, score_ref, cum_ref, row_ref)

    else:
        score_ref, cum_ref, row_ref, par_ref, o_ref = rest
    q_rows = n * fr * 8
    cols = w_ref.shape[0]
    base = head0 + cols // HEAD_DIM * pl.program_id(0)
    skip = widen(par_ref[...], spread_heads(base, cols))[2:3]
    x = dot_nt(x_ref[...], w_ref[...]).astype(BF).astype(F32)
    x = x.reshape(n, m, fr, 2, 8, cols)
    for h in range(m):
        ys = []
        for e in range(2):
            q = 2 * h + e
            xq = x[:, h, :, e].reshape(q_rows, cols)
            cum = pltpu.roll(cum_ref[q], LANES - base, 1)
            y = head_pairs(score_ref.at[q], cum, row_ref, q, base, 0, xq.astype(BF))
            y = y + skip * xq
            ys.append(y.reshape(n, fr, 8, cols))
        o_ref[:, h] = jnp.concatenate(ys, axis=2).astype(BF)


def time_scan(tok_t, w_t, prep, params, head0, heads):
    n = len(tok_t)
    m, fr = tok_t[0].shape[:2]
    per = m * fr * BLK
    rows = n * per
    q_rows = n * fr * 8
    cols = heads * HEAD_DIM
    block = TIME_STEP * HEAD_DIM
    lo = (DI + head0 * HEAD_DIM) // block
    shapes = [(2 * m, q_rows, q_rows), (2 * m, q_rows, LANES), (2 * m, HEADS, q_rows)]
    prep_specs = [full(s) for s in shapes]
    out_specs = [pl.BlockSpec((n, m, fr, BLK, block), lambda j: (0, 0, 0, 0, j))]
    out_shapes = [jax.ShapeDtypeStruct((n, m, fr, BLK, cols), BF)]
    in_specs = [full((per, D))] * n + [pl.BlockSpec((block, D), lambda j: (lo + j, 0))]
    if prep is None:
        in_specs += small_specs(0) + [full(params.shape)]
        args = (w_t, w_t, params)
        out_specs += prep_specs
        out_shapes += [jax.ShapeDtypeStruct(s, F32) for s in shapes]
    else:
        in_specs += prep_specs + [full(params.shape)]
        args = (*prep, params)
    return call(
        functools.partial(time_scan_kernel, n, m, fr, head0, prep is None),
        "time_scan",
        (cols // block,),
        in_specs,
        out_specs,
        out_shapes,
        2 * rows * D * cols + 4 * rows * q_rows * cols,
        2 * (rows * D + D * cols + rows * cols) + 2 * 1024 * 1024,
        scratch=[pltpu.VMEM((rows, D), BF)],
    )(*[piece.reshape(per, D) for piece in tok_t], w_t, *args)


def frame_rows(ref, frame):
    n, m, _, _, cols = ref.shape
    return jnp.concatenate([ref[:, h, frame].reshape(n * BLK, cols) for h in range(m)], axis=0)


def end_of(x, f, tail_ref, b_ref, spread):
    wide = widen_split(tail_ref[f], spread)
    return dot_tn(b_ref[f], (x.astype(F32) * wide).astype(BF)).astype(BF)


def local_of(x, f, head0, score_ref, cum_ref, row_ref, skip):
    y = head_pairs(score_ref.at[f], cum_ref[f], row_ref, f, head0, HEADS + head0, x)
    return y + skip * x.astype(F32)


def space_kernel(head0, npos, local, x_ref, score_ref, cum_ref, row_ref, tail_ref, b_ref, par_ref, *outs):
    spread = spread_heads(head0, x_ref.shape[4])
    skip = widen(par_ref[...], spread)[3:4]
    for f in range(x_ref.shape[2]):
        x = frame_rows(x_ref, f)
        for i, ref in enumerate(outs[local:]):
            own = slice(i * RELAY * HEAD_DIM, i * RELAY * HEAD_DIM + ref.shape[2])
            ref[f] = end_of(x[:, own], f, tail_ref, b_ref, spread[:, own])
        if local:
            outs[0][f] = local_of(x, f, head0, score_ref, cum_ref, row_ref, skip)[:npos]


def space_parts(time_out, space, params, head0, npos, local, end):
    n, m, fr, _, cols = time_out.shape
    size = space[0].shape[1]
    step = 2 if fr % 2 == 0 else 1

    def frames(shape):
        return pl.BlockSpec((step,) + shape, lambda f: (f,) + (0,) * len(shape))

    def unused(shape):
        return pl.BlockSpec(memory_space=pl.ANY)

    l_frames = frames if local else unused
    e_frames = frames if end else unused
    outs = []
    if local:
        outs.append((frames((npos, cols)), jax.ShapeDtypeStruct((fr, npos, cols), F32)))
    if end:
        width = RELAY * HEAD_DIM
        for at in range(0, cols, width):
            piece = min(width, cols - at)
            outs.append((frames((STATE, piece)), jax.ShapeDtypeStruct((fr, STATE, piece), BF)))
    return call(
        functools.partial(space_kernel, head0, npos, local),
        "space" + "_local" * local + "_end" * end,
        (fr // step,),
        [
            pl.BlockSpec((n, m, step, BLK, cols), lambda f: (0, 0, f, 0, 0)),
            l_frames((size, size)),
            l_frames((size, LANES)),
            l_frames((HEADS, size)),
            e_frames((size, 2 * LANES)),
            e_frames((size, STATE)),
            full(params.shape),
        ],
        [spec for spec, _ in outs],
        [shape for _, shape in outs],
        4 * fr * size * size * cols,
        6 * fr * size * cols + 2 * 1024 * 1024,
    )(time_out, *space, params)


def gated_of(local, z, ecum_ref, c_ref, spread, states):
    state = sum(ref[0].astype(F32) for ref in states)
    npos = local.shape[0]
    carried = dot(c_ref[0], state.astype(BF))[:npos]
    wide = widen_split(ecum_ref[0], spread)[:npos]
    z = z.astype(F32)
    return (local + wide * carried) * (0.5 * z * (1.0 + jnp.tanh(0.5 * z)))


def lane_sums(v):
    return sum(v[:, a : a + LANES] for a in range(0, v.shape[1], LANES))


def finish_heads(cuts, locals_, states, z_ref, ecum_ref, c_ref, gain_ref, w_ref):
    total, squares, used = None, None, 0
    base = cuts[0][0]
    for local, (lo, hi) in zip(locals_, cuts):
        pieces = -(-(hi - lo) // (RELAY * HEAD_DIM))
        hops = len(states) // sum(-(-(b - a) // (RELAY * HEAD_DIM)) for a, b in cuts)
        for p in range(pieces):
            at, to = lo + p * RELAY * HEAD_DIM, min(hi, lo + (p + 1) * RELAY * HEAD_DIM)
            own = slice(at - base, to - base)
            gated = gated_of(
                local[0, :, at - lo : to - lo],
                z_ref[0, :, own],
                ecum_ref,
                c_ref,
                spread_heads(at // HEAD_DIM, to - at),
                states[used : used + hops],
            )
            used += hops
            part = dot((gated * gain_ref[:, own]).astype(BF), w_ref[own])
            square = lane_sums(gated * gated)
            total = part if total is None else total + part
            squares = square if squares is None else squares + square
    return total, squares


def early_kernel(cuts, z_ref, ecum_ref, c_ref, gain_ref, w_ref, *rest):
    count = len(cuts)
    locals_, states, (o_ref, sq_ref) = rest[:count], rest[count:-2], rest[-2:]
    o_ref[0], sq_ref[0] = finish_heads(cuts, locals_, states, z_ref, ecum_ref, c_ref, gain_ref, w_ref)


def last_kernel(cuts, z_ref, ecum_ref, c_ref, gain_ref, w_ref, acc_ref, sq_ref, tok_ref, *rest):
    count = len(cuts)
    locals_, states, o_ref = rest[:count], rest[count:-1], rest[-1]
    total, squares = finish_heads(cuts, locals_, states, z_ref, ecum_ref, c_ref, gain_ref, w_ref)
    mean = jnp.sum(squares + sq_ref[0], axis=1, keepdims=True) * (1.0 / DI)
    inv_scale = lax.rsqrt(mean + 1e-05)
    o_ref[0] = ((total + acc_ref[0]) * inv_scale + tok_ref[0].astype(F32)).astype(BF)


def finish(cuts, locals_, states, gate, ecum, c, gain, w_out, before=None):
    fr, npos, _ = gate.shape
    size = c.shape[1]
    cols = cuts[-1][1] - cuts[0][0]
    own = cuts[0][0] // cols
    per_frame = lambda f: (f, 0, 0)
    wide, narrow = pl.BlockSpec((1, npos, D), per_frame), pl.BlockSpec((1, npos, LANES), per_frame)
    in_specs = [
        pl.BlockSpec((1, npos, cols), lambda f: (f, 0, own)),
        pl.BlockSpec((1, size, 2 * LANES), per_frame),
        pl.BlockSpec((1, size, STATE), per_frame),
        pl.BlockSpec((1, cols), lambda f: (0, own)),
        pl.BlockSpec((cols, D), lambda f: (own, 0)),
    ]
    if before is None:
        kernel, before, name = early_kernel, (), "early"
        out_specs = [wide, narrow]
        out_shape = [
            jax.ShapeDtypeStruct((fr, npos, D), F32),
            jax.ShapeDtypeStruct((fr, npos, LANES), F32),
        ]
    else:
        kernel, name = last_kernel, "last"
        in_specs += [wide, narrow, wide]
        out_specs, out_shape = wide, jax.ShapeDtypeStruct((fr, npos, D), BF)
    return call(
        functools.partial(kernel, cuts),
        name,
        (fr,),
        in_specs + [pl.BlockSpec((1,) + v.shape[1:], per_frame) for v in (*locals_, *states)],
        out_specs,
        out_shape,
        2 * fr * npos * cols * D,
        8 * fr * npos * cols + 2 * cols * D + 4 * fr * npos * D,
        vmem=VMEM_TAIL,
    )(gate, ecum, c, gain, w_out, *before, *locals_, *states)


def hop(state, k):
    return lax.ppermute(state, "space", [(k, k + 1)])


def join(end, growth, start):
    return (end.astype(F32) + growth * start.astype(F32)).astype(BF)


def after(value, other):
    return lax.optimization_barrier((value, other))[0]


def body(
    tokens, w_in, w_out, a_log_time, a_log_space, dt_bias_time, dt_bias_space, skip_time, skip_space, norm_gain
):
    fr, rows_dev, cols_dev, _ = tokens.shape
    n = lax.axis_size("tm")
    npos = rows_dev * cols_dev
    m = -(-(npos // BLK) // n)
    size = m * n * BLK
    tok = tokens.reshape(fr, npos, D)
    flat = tokens.reshape(fr * npos, D)

    tok_t = exchange(arrange(tok, n, m))

    w_t = w_in.T
    fill = jnp.zeros((LANES - 2 * HEADS,), F32)
    none = jnp.zeros((HEADS,), F32)
    params = jnp.stack(
        [
            jnp.concatenate([dt_bias_time, dt_bias_space, fill]),
            jnp.concatenate([-jnp.exp(a_log_time) * LOG2E, -jnp.exp(a_log_space) * LOG2E, fill]),
            jnp.concatenate([none, skip_time, fill]),
            jnp.concatenate([none, skip_space, fill]),
        ]
        + [jnp.zeros((LANES,), F32)] * 4
    )
    gain = norm_gain[None]

    gate = gate_proj(flat, w_t).reshape(fr, npos, DI)
    score, cum, row, tail, ecum, b, c, growth = space_prep(tok, w_t, params, size)
    tok_t, gate, growth = lax.optimization_barrier((tok_t, gate, growth))

    starts = [sum(GROUPS[:i]) for i in range(len(GROUPS))]
    space = (score, cum, row, tail, b)
    prep = None
    outs = []
    for head0, heads in zip(starts, GROUPS):
        out, *made = time_scan(tok_t, w_t, prep, params, head0, heads)
        prep = prep or made
        outs.append(out)
    hops = lax.axis_size("space") - 1
    locals_, cuts, ends, grows, states = [], [], [], [], []

    def send(i, k, beside):
        moving = ends[i]
        if k:
            got = after(states[i][k - 1], beside)
            moving = [join(e, g, r) for e, g, r in zip(ends[i], grows[i], got)]
        states[i].append([hop(e, k) for e in moving])
        return moving

    for i, head0 in enumerate(starts):
        arrived = lax.all_to_all(outs[i], "tm", split_axis=0, concat_axis=0, tiled=True)
        arrived, outs[i + 1 :] = after((arrived, outs[i + 1 :]), ends[-1:])
        lo, hi = head0 * HEAD_DIM, (head0 + GROUPS[i]) * HEAD_DIM
        local, *end = space_parts(arrived, space, params, head0, npos, True, True)
        locals_.append(local)
        cuts.append((lo, hi))
        ends.append(end)
        width = RELAY * HEAD_DIM
        grows.append([growth[:, :, at : min(hi, at + width)] for at in range(lo, hi, width)])
        states.append([])
        moved = send(i, 0, None)
        for j in range(i):
            if i - j <= hops - 1:
                moved = moved + send(j, i - j, end)
    while any(len(hopped) < hops for hopped in states):
        for j, hopped in enumerate(states):
            if len(hopped) < hops:
                moved = send(j, len(hopped), None)
    flat_states = lambda a, b: [r[p] for i in range(a, b) for p in range(len(ends[i])) for r in states[i]]
    acc, squares = finish(
        cuts[:EARLY], locals_[:EARLY], flat_states(0, EARLY), after(gate, moved), ecum, c, gain, w_out
    )
    out = finish(
        cuts[EARLY:],
        locals_[EARLY:],
        flat_states(EARLY, len(GROUPS)),
        gate,
        ecum,
        c,
        gain,
        w_out,
        (acc, squares, tok),
    )
    return out.reshape(tokens.shape)


def solution(mesh):
    placed = (P("tm", "space", None, None), P(), P(), P(), P(), P(), P(), P(), P(), P())
    return jax.shard_map(
        body, mesh=mesh, in_specs=placed, out_specs=P("tm", "space", None, None), check_vma=False
    )
```

```python
import functools

import jax
import jax.numpy as jnp
from jax import lax
from jax.experimental import pallas as pl
from jax.experimental.pallas import tpu as pltpu
from jax.sharding import PartitionSpec as P

D = 1024
HEADS = 32
HEAD_DIM = 64
STATE = 64
DI = 2048
BLK = 16
LANES = 128
LOG2E = 1.4426950408889634
TOP = 64.0
GROUPS = (16, 8, 8)
RELAY = 16
EARLY = 1
TIME_STEP = 8
BF = jnp.bfloat16
F32 = jnp.float32
VMEM = 58 * 1024 * 1024
VMEM_TAIL = 40 * 1024 * 1024


def call(kernel, name, grid, in_specs, out_specs, out_shape, flops, moved, scratch=(), vmem=VMEM):
    return pl.pallas_call(
        kernel,
        name=name,
        grid=grid,
        in_specs=in_specs,
        out_specs=out_specs,
        out_shape=out_shape,
        scratch_shapes=scratch,
        compiler_params=pltpu.CompilerParams(vmem_limit_bytes=vmem),
        cost_estimate=pl.CostEstimate(flops=flops, bytes_accessed=moved, transcendentals=0),
    )


def dot(a, b):
    return jnp.dot(a, b, preferred_element_type=F32)


def dot_nt(a, b):
    return lax.dot_general(a, b, (((1,), (1,)), ((), ())), preferred_element_type=F32)


def dot_tn(a, b):
    return lax.dot_general(a, b, (((0,), (0,)), ((), ())), preferred_element_type=F32)


def softplus(x):
    return jnp.maximum(x, 0.0) + jnp.log1p(jnp.exp(-jnp.abs(x)))


def spread_heads(head0, cols):
    row = lax.broadcasted_iota(jnp.int32, (LANES, cols), 0)
    col = lax.broadcasted_iota(jnp.int32, (LANES, cols), 1)
    return jnp.where(row - HEADS - head0 == col // HEAD_DIM, 1.0, 0.0).astype(BF)


def split2(v):
    high = v.astype(BF)
    return jnp.concatenate([high, (v - high.astype(F32)).astype(BF)], axis=1)


def widen_split(parts, spread):
    return dot(parts, jnp.concatenate([spread, spread], axis=0))


def widen(values, spread):
    return widen_split(split2(values), spread)


def full(shape):
    return pl.BlockSpec(shape, lambda *_: (0,) * len(shape))


def arrange_kernel(n, x_ref, *outs):
    rows = x_ref.shape[1]
    for k, o_ref in enumerate(outs):
        to = jnp.bitwise_xor(lax.axis_index("tm"), k)
        for h in range(o_ref.shape[0]):
            at = (h * n + to) * BLK
            start = pl.multiple_of(jnp.minimum(at, rows - BLK), BLK)
            o_ref[h] = x_ref[:, pl.ds(start, BLK), :]

            @pl.when(at >= rows)
            def _():
                o_ref[h] = jnp.zeros(o_ref.shape[1:], BF)


def arrange(tok, n, m):
    fr, npos, _ = tok.shape
    step = 2 if fr % 2 == 0 else 1
    return call(
        functools.partial(arrange_kernel, n),
        "arrange",
        (fr // step,),
        [pl.BlockSpec((step, npos, D), lambda f: (f, 0, 0))],
        [pl.BlockSpec((m, step, BLK, D), lambda f: (0, f, 0, 0))] * n,
        [jax.ShapeDtypeStruct((m, fr, BLK, D), BF)] * n,
        0,
        4 * fr * npos * D,
    )(tok)


def exchange(pieces):
    n = len(pieces)
    order = [k for k in range(n - 1, 1, -1)] + [1]
    got = {k: lax.ppermute(pieces[k], "tm", [(i, i ^ k) for i in range(n)]) for k in order}
    return [pieces[0]] + [got[k] for k in range(1, n)]


def gate_kernel(x_ref, w_ref, o_ref):
    o_ref[...] = dot_nt(x_ref[...], w_ref[...]).astype(BF)


def gate_proj(flat, w_t):
    rows = flat.shape[0]
    return call(
        gate_kernel,
        "gate_proj",
        (2,),
        [full((rows, D)), pl.BlockSpec((DI // 2, D), lambda j: (j, 0))],
        pl.BlockSpec((rows, DI // 2), lambda j: (0, j)),
        jax.ShapeDtypeStruct((rows, DI), BF),
        2 * rows * D * DI,
        2 * (rows * D + D * DI + rows * DI),
    )(flat, w_t)


def small_proj(x, w_ref, raw_w_ref):
    raw = dot_nt(x, raw_w_ref[...])
    zeros = jnp.zeros((raw.shape[0], LANES - raw.shape[1]), F32)
    return dot_nt(x, w_ref[...]), jnp.concatenate([raw, zeros], axis=1)


def small_specs(group):
    first = 2 * DI // LANES + group
    raw = (2 * DI + 4 * STATE) // (2 * HEADS)
    return [
        pl.BlockSpec((LANES, D), lambda *_: (first, 0)),
        pl.BlockSpec((2 * HEADS, D), lambda *_: (raw, 0)),
    ]


def space_prep_kernel(
    npos, x_ref, w_ref, raw_w_ref, par_ref, score_ref, cum_ref, row_ref, tail_ref, ecum_ref, b_ref, c_ref, grow_ref
):
    size = score_ref.shape[1]
    bc, raw = small_proj(x_ref[0], w_ref, raw_w_ref)
    pad = jnp.zeros((size - npos, LANES), F32)
    bc = jnp.concatenate([bc.astype(BF).astype(F32), pad], axis=0)
    b = bc[:, :STATE].astype(BF)
    c = bc[:, STATE:].astype(BF)
    step = softplus(raw + par_ref[0:1])
    step = jnp.concatenate([step, pad], axis=0)
    dec = step * par_ref[1:2]
    ri = lax.broadcasted_iota(jnp.int32, (size, size), 0)
    ci = lax.broadcasted_iota(jnp.int32, (size, size), 1)
    causal = ri >= ci
    cum = jnp.dot(
        causal.astype(F32), dec, precision=lax.Precision.HIGHEST, preferred_element_type=F32
    )
    total = cum[npos - 1 : npos]
    rowterm = jnp.log2(step) - cum
    score_ref[0] = jnp.where(causal, dot_nt(c, b), 0.0)
    cum_ref[0] = cum
    row_ref[0] = rowterm.T[HEADS : 2 * HEADS]
    tail = jnp.exp2(jnp.minimum(total + rowterm, TOP))
    tail_ref[0] = split2(tail)
    ecum_ref[0] = split2(jnp.exp2(cum))
    b_ref[0] = b
    c_ref[0] = c
    growth = jnp.broadcast_to(jnp.exp2(total), (8, LANES))
    grow_ref[0] = widen(growth, spread_heads(0, DI))[0:1]


def space_prep(tok, w_t, params, size):
    fr, npos, _ = tok.shape

    def per_frame(shape):
        return pl.BlockSpec((1,) + shape, lambda f: (f,) + (0,) * len(shape))

    shapes = [
        ((size, size), F32),
        ((size, LANES), F32),
        ((HEADS, size), F32),
        ((size, 2 * LANES), BF),
        ((size, 2 * LANES), BF),
        ((size, STATE), BF),
        ((size, STATE), BF),
        ((1, DI), F32),
    ]
    return call(
        functools.partial(space_prep_kernel, npos),
        "space_prep",
        (fr,),
        [per_frame((npos, D))] + small_specs(1) + [full(params.shape)],
        [per_frame(s) for s, _ in shapes],
        [jax.ShapeDtypeStruct((fr,) + s, t) for s, t in shapes],
        2 * fr * npos * D * 256,
        6 * 1024 * 1024,
    )(tok, w_t, w_t, params)


def time_prep(n, m, fr, x, w_ref, raw_w_ref, par_ref, score_ref, cum_ref, row_ref):
    bc, raw = small_proj(x, w_ref, raw_w_ref)
    shape = (n, m, fr, 2, 8, LANES)
    q_rows = n * fr * 8
    bc = bc.astype(BF).astype(F32).reshape(shape)
    step = softplus(raw.astype(BF).astype(F32) + par_ref[0:1])
    dec = (step * par_ref[1:2]).reshape(shape)
    step = step.reshape(shape)
    ri = lax.broadcasted_iota(jnp.int32, (q_rows, q_rows), 0)
    ci = lax.broadcasted_iota(jnp.int32, (q_rows, q_rows), 1)
    keep = (ri >= ci) & ((ri & 7) == (ci & 7))
    for h in range(m):
        for e in range(2):
            q = 2 * h + e
            running = jnp.zeros((8, LANES), F32)
            parts = []
            for s in range(n):
                for f in range(fr):
                    running = running + dec[s, h, f, e]
                    parts.append(running)
            cum = jnp.concatenate(parts, axis=0)
            bcq = bc[:, h, :, e].reshape(q_rows, LANES)
            b = bcq[:, :STATE].astype(BF)
            c = bcq[:, STATE:].astype(BF)
            score_ref[q] = jnp.where(keep, dot_nt(c, b), 0.0)
            cum_ref[q] = cum
            rowterm = jnp.log2(step[:, h, :, e].reshape(q_rows, LANES)) - cum
            row_ref[q] = rowterm.T[:HEADS]


def head_pair(score, cum, row, x_pair):
    rows = x_pair.shape[0]
    lane = lax.broadcasted_iota(jnp.int32, (1, LANES), 1)
    left = jnp.where(lane < HEAD_DIM, 1.0, 0.0).astype(BF)
    halves = (x_pair * left, x_pair * (1 - left))
    cols = [jnp.broadcast_to(c, (rows, LANES)) for c in cum]
    out = [None] * (rows // LANES)
    for j in range(rows // LANES):
        lo, hi = j * LANES, (j + 1) * LANES
        pieces = []
        for k in range(2):
            span = cols[k][lo:] + row[k][:, lo:hi]
            pieces.append((jnp.exp2(jnp.minimum(span, TOP)) * score[lo:, lo:hi]).astype(BF))
        keys = jnp.concatenate([halves[0][lo:hi], halves[1][lo:hi]], axis=0)
        part = dot(jnp.concatenate(pieces, axis=1), keys)
        for i in range(j, rows // LANES):
            block = part[(i - j) * LANES : (i - j + 1) * LANES]
            out[i] = block if out[i] is None else out[i] + block
    return jnp.concatenate(out, axis=0)


def head_pairs(score, cum, row_ref, row_at, head0, lane0, x):
    ys = []
    for p in range(x.shape[1] // LANES):
        pair = (2 * p, 2 * p + 1)
        ys.append(
            head_pair(
                score,
                [cum[:, lane0 + k : lane0 + k + 1] for k in pair],
                [row_ref[row_at, pl.ds(head0 + k, 1), :] for k in pair],
                x[:, p * LANES : (p + 1) * LANES],
            )
        )
    return jnp.concatenate(ys, axis=1)


def time_scan_kernel(n, m, fr, head0, first, *refs):
    pieces, w_ref, rest, x_ref = refs[:n], refs[n], refs[n + 1 : -1], refs[-1]

    @pl.when(pl.program_id(0) == 0)
    def _():
        per = m * fr * BLK
        for k, ref in enumerate(pieces):
            source = jnp.bitwise_xor(lax.axis_index("tm"), k)
            x_ref[pl.ds(pl.multiple_of(source * per, per), per), :] = ref[...]

    if first:
        small, (par_ref, o_ref, score_ref, cum_ref, row_ref) = rest[:2], rest[2:]

        @pl.when(pl.program_id(0) == 0)
        def _():
            time_prep(n, m, fr, x_ref[...], *small, par_ref, score_ref, cum_ref, row_ref)

    else:
        score_ref, cum_ref, row_ref, par_ref, o_ref = rest
    q_rows = n * fr * 8
    cols = w_ref.shape[0]
    base = head0 + cols // HEAD_DIM * pl.program_id(0)
    skip = widen(par_ref[...], spread_heads(base, cols))[2:3]
    x = dot_nt(x_ref[...], w_ref[...]).astype(BF).astype(F32)
    x = x.reshape(n, m, fr, 2, 8, cols)
    for h in range(m):
        ys = []
        for e in range(2):
            q = 2 * h + e
            xq = x[:, h, :, e].reshape(q_rows, cols)
            cum = pltpu.roll(cum_ref[q], LANES - base, 1)
            y = head_pairs(score_ref.at[q], cum, row_ref, q, base, 0, xq.astype(BF))
            y = y + skip * xq
            ys.append(y.reshape(n, fr, 8, cols))
        o_ref[:, h] = jnp.concatenate(ys, axis=2).astype(BF)


def time_scan(tok_t, w_t, prep, params, head0, heads):
    n = len(tok_t)
    m, fr = tok_t[0].shape[:2]
    per = m * fr * BLK
    rows = n * per
    q_rows = n * fr * 8
    cols = heads * HEAD_DIM
    block = TIME_STEP * HEAD_DIM
    lo = (DI + head0 * HEAD_DIM) // block
    shapes = [(2 * m, q_rows, q_rows), (2 * m, q_rows, LANES), (2 * m, HEADS, q_rows)]
    prep_specs = [full(s) for s in shapes]
    out_specs = [pl.BlockSpec((n, m, fr, BLK, block), lambda j: (0, 0, 0, 0, j))]
    out_shapes = [jax.ShapeDtypeStruct((n, m, fr, BLK, cols), BF)]
    in_specs = [full((per, D))] * n + [pl.BlockSpec((block, D), lambda j: (lo + j, 0))]
    if prep is None:
        in_specs += small_specs(0) + [full(params.shape)]
        args = (w_t, w_t, params)
        out_specs += prep_specs
        out_shapes += [jax.ShapeDtypeStruct(s, F32) for s in shapes]
    else:
        in_specs += prep_specs + [full(params.shape)]
        args = (*prep, params)
    return call(
        functools.partial(time_scan_kernel, n, m, fr, head0, prep is None),
        "time_scan",
        (cols // block,),
        in_specs,
        out_specs,
        out_shapes,
        2 * rows * D * cols + 4 * rows * q_rows * cols,
        2 * (rows * D + D * cols + rows * cols) + 2 * 1024 * 1024,
        scratch=[pltpu.VMEM((rows, D), BF)],
    )(*[piece.reshape(per, D) for piece in tok_t], w_t, *args)


def frame_rows(ref, frame):
    n, m, _, _, cols = ref.shape
    return jnp.concatenate([ref[:, h, frame].reshape(n * BLK, cols) for h in range(m)], axis=0)


def end_of(x, f, tail_ref, b_ref, spread):
    wide = widen_split(tail_ref[f], spread)
    return dot_tn(b_ref[f], (x.astype(F32) * wide).astype(BF)).astype(BF)


def local_of(x, f, head0, score_ref, cum_ref, row_ref, skip):
    y = head_pairs(score_ref.at[f], cum_ref[f], row_ref, f, head0, HEADS + head0, x)
    return y + skip * x.astype(F32)


def space_kernel(head0, npos, local, x_ref, score_ref, cum_ref, row_ref, tail_ref, b_ref, par_ref, *outs):
    spread = spread_heads(head0, x_ref.shape[4])
    skip = widen(par_ref[...], spread)[3:4]
    for f in range(x_ref.shape[2]):
        x = frame_rows(x_ref, f)
        for i, ref in enumerate(outs[local:]):
            own = slice(i * RELAY * HEAD_DIM, i * RELAY * HEAD_DIM + ref.shape[2])
            ref[f] = end_of(x[:, own], f, tail_ref, b_ref, spread[:, own])
        if local:
            outs[0][f] = local_of(x, f, head0, score_ref, cum_ref, row_ref, skip)[:npos]


def space_parts(time_out, space, params, head0, npos, local, end):
    n, m, fr, _, cols = time_out.shape
    size = space[0].shape[1]
    step = 2 if fr % 2 == 0 else 1

    def frames(shape):
        return pl.BlockSpec((step,) + shape, lambda f: (f,) + (0,) * len(shape))

    def unused(shape):
        return pl.BlockSpec(memory_space=pl.ANY)

    l_frames = frames if local else unused
    e_frames = frames if end else unused
    outs = []
    if local:
        outs.append((frames((npos, cols)), jax.ShapeDtypeStruct((fr, npos, cols), F32)))
    if end:
        width = RELAY * HEAD_DIM
        for at in range(0, cols, width):
            piece = min(width, cols - at)
            outs.append((frames((STATE, piece)), jax.ShapeDtypeStruct((fr, STATE, piece), BF)))
    return call(
        functools.partial(space_kernel, head0, npos, local),
        "space" + "_local" * local + "_end" * end,
        (fr // step,),
        [
            pl.BlockSpec((n, m, step, BLK, cols), lambda f: (0, 0, f, 0, 0)),
            l_frames((size, size)),
            l_frames((size, LANES)),
            l_frames((HEADS, size)),
            e_frames((size, 2 * LANES)),
            e_frames((size, STATE)),
            full(params.shape),
        ],
        [spec for spec, _ in outs],
        [shape for _, shape in outs],
        4 * fr * size * size * cols,
        6 * fr * size * cols + 2 * 1024 * 1024,
    )(time_out, *space, params)


def gated_of(local, z, ecum_ref, c_ref, spread, states):
    state = sum(ref[0].astype(F32) for ref in states)
    npos = local.shape[0]
    carried = dot(c_ref[0], state.astype(BF))[:npos]
    wide = widen_split(ecum_ref[0], spread)[:npos]
    z = z.astype(F32)
    return (local + wide * carried) * (0.5 * z * (1.0 + jnp.tanh(0.5 * z)))


def lane_sums(v):
    return sum(v[:, a : a + LANES] for a in range(0, v.shape[1], LANES))


def finish_heads(cuts, locals_, states, z_ref, ecum_ref, c_ref, gain_ref, w_ref):
    total, squares, used = None, None, 0
    base = cuts[0][0]
    for local, (lo, hi) in zip(locals_, cuts):
        pieces = -(-(hi - lo) // (RELAY * HEAD_DIM))
        hops = len(states) // sum(-(-(b - a) // (RELAY * HEAD_DIM)) for a, b in cuts)
        for p in range(pieces):
            at, to = lo + p * RELAY * HEAD_DIM, min(hi, lo + (p + 1) * RELAY * HEAD_DIM)
            own = slice(at - base, to - base)
            gated = gated_of(
                local[0, :, at - lo : to - lo],
                z_ref[0, :, own],
                ecum_ref,
                c_ref,
                spread_heads(at // HEAD_DIM, to - at),
                states[used : used + hops],
            )
            used += hops
            part = dot((gated * gain_ref[:, own]).astype(BF), w_ref[own])
            square = lane_sums(gated * gated)
            total = part if total is None else total + part
            squares = square if squares is None else squares + square
    return total, squares


def early_kernel(cuts, z_ref, ecum_ref, c_ref, gain_ref, w_ref, *rest):
    count = len(cuts)
    locals_, states, (o_ref, sq_ref) = rest[:count], rest[count:-2], rest[-2:]
    o_ref[0], sq_ref[0] = finish_heads(cuts, locals_, states, z_ref, ecum_ref, c_ref, gain_ref, w_ref)


def last_kernel(cuts, z_ref, ecum_ref, c_ref, gain_ref, w_ref, acc_ref, sq_ref, tok_ref, *rest):
    count = len(cuts)
    locals_, states, o_ref = rest[:count], rest[count:-1], rest[-1]
    total, squares = finish_heads(cuts, locals_, states, z_ref, ecum_ref, c_ref, gain_ref, w_ref)
    mean = jnp.sum(squares + sq_ref[0], axis=1, keepdims=True) * (1.0 / DI)
    inv_scale = lax.rsqrt(mean + 1e-05)
    o_ref[0] = ((total + acc_ref[0]) * inv_scale + tok_ref[0].astype(F32)).astype(BF)


def finish(cuts, locals_, states, gate, ecum, c, gain, w_out, before=None):
    fr, npos, _ = gate.shape
    size = c.shape[1]
    cols = cuts[-1][1] - cuts[0][0]
    own = cuts[0][0] // cols
    per_frame = lambda f: (f, 0, 0)
    wide, narrow = pl.BlockSpec((1, npos, D), per_frame), pl.BlockSpec((1, npos, LANES), per_frame)
    in_specs = [
        pl.BlockSpec((1, npos, cols), lambda f: (f, 0, own)),
        pl.BlockSpec((1, size, 2 * LANES), per_frame),
        pl.BlockSpec((1, size, STATE), per_frame),
        pl.BlockSpec((1, cols), lambda f: (0, own)),
        pl.BlockSpec((cols, D), lambda f: (own, 0)),
    ]
    if before is None:
        kernel, before, name = early_kernel, (), "early"
        out_specs = [wide, narrow]
        out_shape = [
            jax.ShapeDtypeStruct((fr, npos, D), F32),
            jax.ShapeDtypeStruct((fr, npos, LANES), F32),
        ]
    else:
        kernel, name = last_kernel, "last"
        in_specs += [wide, narrow, wide]
        out_specs, out_shape = wide, jax.ShapeDtypeStruct((fr, npos, D), BF)
    return call(
        functools.partial(kernel, cuts),
        name,
        (fr,),
        in_specs + [pl.BlockSpec((1,) + v.shape[1:], per_frame) for v in (*locals_, *states)],
        out_specs,
        out_shape,
        2 * fr * npos * cols * D,
        8 * fr * npos * cols + 2 * cols * D + 4 * fr * npos * D,
        vmem=VMEM_TAIL,
    )(gate, ecum, c, gain, w_out, *before, *locals_, *states)


def hop(state, k):
    return lax.ppermute(state, "space", [(k, k + 1)])


def join(end, growth, start):
    return (end.astype(F32) + growth * start.astype(F32)).astype(BF)


def after(value, other):
    return lax.optimization_barrier((value, other))[0]


def body(
    tokens, w_in, w_out, a_log_time, a_log_space, dt_bias_time, dt_bias_space, skip_time, skip_space, norm_gain
):
    fr, rows_dev, cols_dev, _ = tokens.shape
    n = lax.axis_size("tm")
    npos = rows_dev * cols_dev
    m = -(-(npos // BLK) // n)
    size = m * n * BLK
    tok = tokens.reshape(fr, npos, D)
    flat = tokens.reshape(fr * npos, D)

    tok_t = exchange(arrange(tok, n, m))

    w_t = w_in.T
    fill = jnp.zeros((LANES - 2 * HEADS,), F32)
    none = jnp.zeros((HEADS,), F32)
    params = jnp.stack(
        [
            jnp.concatenate([dt_bias_time, dt_bias_space, fill]),
            jnp.concatenate([-jnp.exp(a_log_time) * LOG2E, -jnp.exp(a_log_space) * LOG2E, fill]),
            jnp.concatenate([none, skip_time, fill]),
            jnp.concatenate([none, skip_space, fill]),
        ]
        + [jnp.zeros((LANES,), F32)] * 4
    )
    gain = norm_gain[None]

    gate = gate_proj(flat, w_t).reshape(fr, npos, DI)
    score, cum, row, tail, ecum, b, c, growth = space_prep(tok, w_t, params, size)
    tok_t, gate, growth = lax.optimization_barrier((tok_t, gate, growth))

    starts = [sum(GROUPS[:i]) for i in range(len(GROUPS))]
    space = (score, cum, row, tail, b)
    prep = None
    outs = []
    for head0, heads in zip(starts, GROUPS):
        out, *made = time_scan(tok_t, w_t, prep, params, head0, heads)
        prep = prep or made
        outs.append(out)
    hops = lax.axis_size("space") - 1
    locals_, cuts, ends, grows, states = [], [], [], [], []

    def send(i, k, beside):
        moving = ends[i]
        if k:
            got = after(states[i][k - 1], beside)
            moving = [join(e, g, r) for e, g, r in zip(ends[i], grows[i], got)]
        states[i].append([hop(e, k) for e in moving])
        return moving

    for i, head0 in enumerate(starts):
        arrived = lax.all_to_all(outs[i], "tm", split_axis=0, concat_axis=0, tiled=True)
        arrived, outs[i + 1 :] = after((arrived, outs[i + 1 :]), ends[-1:])
        lo, hi = head0 * HEAD_DIM, (head0 + GROUPS[i]) * HEAD_DIM
        local, *end = space_parts(arrived, space, params, head0, npos, True, True)
        locals_.append(local)
        cuts.append((lo, hi))
        ends.append(end)
        width = RELAY * HEAD_DIM
        grows.append([growth[:, :, at : min(hi, at + width)] for at in range(lo, hi, width)])
        states.append([])
        moved = send(i, 0, None)
        for j in range(i):
            if i - j <= hops - 1:
                moved = moved + send(j, i - j, end)
    while any(len(hopped) < hops for hopped in states):
        for j, hopped in enumerate(states):
            if len(hopped) < hops:
                moved = send(j, len(hopped), None)
    flat_states = lambda a, b: [r[p] for i in range(a, b) for p in range(len(ends[i])) for r in states[i]]
    acc, squares = finish(
        cuts[:EARLY], locals_[:EARLY], flat_states(0, EARLY), after(gate, moved), ecum, c, gain, w_out
    )
    out = finish(
        cuts[EARLY:],
        locals_[EARLY:],
        flat_states(EARLY, len(GROUPS)),
        gate,
        ecum,
        c,
        gain,
        w_out,
        (acc, squares, tok),
    )
    return out.reshape(tokens.shape)


def solution(mesh):
    placed = (P("tm", "space", None, None), P(), P(), P(), P(), P(), P(), P(), P(), P())
    return jax.shard_map(
        body, mesh=mesh, in_specs=placed, out_specs=P("tm", "space", None, None), check_vma=False
    )
```
